512 devices in a mesh: sect: 2 (over core), grp: 32 (over z_hi, x, y), seq: 8 (over z_lo).
Axes of the slice: x: 4, y: 4, z: 16 (z_hi: 2, z_lo: 8; z = z_hi * 8 + z_lo), core: 2. Of those that a mesh axis runs over, the one named last changes fastest.
Arguments:
- qkv_img: bfloat16 [32, 2048, 3, 2048], P('grp', ('sect', 'seq')), may hold values from -60 to 60
- img_seg: int32 [32, 2048], P('grp', ('sect', 'seq')), may hold values from 0 to 3, never falling along the last dimension, each value on 1 to 1024 neighbouring positions
- text_kv: bfloat16 [128, 2, 64, 2048], P('grp', None, None, ('sect', 'seq')), may hold values from -6 to 6
- txt_len: int32 [128], P('grp'), may hold values from 1 to 64
- req_slot: int32 [128], P('grp'), may hold values from 0 to 127, each once
Outputs:
- attn_out: bfloat16 [32, 2048, 2048], P('grp', ('sect', 'seq'))
The draws below stay inside these ranges and needn't reach their ends.
Inputs may be any that keep to these rules, and one draw needn't show every extreme that they name: Request r goes to group req_slot[r] // 4 as its slot req_slot[r] % 4.
All inputs are finite; a program needn't handle non-finite values.
Results may differ from the reference program's by a relative error of at most 0.008.
Values may be sent and summed in bfloat16 or wider, within the bound.
A program may use at most 128 MiB of HBM per device.

```python
import math
import jax
import jax.numpy as jnp
import numpy as np
from jax import lax

HEADS = 16
HD = 128
REQ_G = 4
TXT = 64
GROUPS = 32
SEQ_LEN = 2048
REQUESTS = 128


def draw_txt_len(key, part):
    key = jax.random.fold_in(key, 7)
    counts = jax.random.randint(key, (REQUESTS,), 1, TXT + 1, dtype=jnp.int32)
    return counts.at[0].set(TXT)


def draw_qkv_img(key, part):
    key = jax.random.fold_in(key, 11)
    first_key = jax.random.fold_in(key, 0)
    shape = (GROUPS, SEQ_LEN, 3, HEADS * HD)
    base = jnp.clip(jax.random.normal(first_key, shape, jnp.float32), -6.0, 6.0)
    return base.astype(jnp.bfloat16)


def level_of(own_key, shape, cuts, least, largest):
    def one(axis_at, blocks):
        steps = jax.random.uniform(jax.random.fold_in(jax.random.fold_in(own_key, 6), axis_at), (blocks,), jnp.float32, least / len(cuts), largest / len(cuts))
        return jnp.repeat(jnp.exp(steps), shape[axis_at] // blocks).reshape((-1,) + (1,) * (len(shape) - axis_at - 1))

    gain = one(*cuts[0])
    for cut in cuts[1:]:
        gain = gain * one(*cut)
    return gain


def length_profile(amount, total, most, slope):
    loads = [(1 << 20) // math.isqrt(standing ** slope) + 1 for standing in range(2, amount + 1)]
    spare, given = total - most - (amount - 1), [1] * (amount - 1)
    while spare > 0:
        free = [i for i in range(amount - 1) if given[i] < most]
        whole, remaining = sum([loads[i] for i in free]), spare
        for i in free:
            addition = min(most - given[i], max(1, remaining * loads[i] // whole), spare)
            given[i] = given[i] + addition
            spare = spare - addition
    return np.array([most] + given)


def ragged_sizes(rng, count, total, reach, lean):
    if count == 2:
        one = jax.random.randint(rng, (), max(1, total - reach), min(reach, total - 1) + 1)
        return jnp.stack([one, total - one])
    sizes = jnp.asarray(length_profile(count, total, reach, lean), jnp.int32)
    pairs = (count - 1) // 2
    donor, receiver = sizes[1:1 + 2 * pairs:2], sizes[2:2 + 2 * pairs:2]
    room = jnp.minimum(donor - 1, reach - receiver)
    shifted = jax.random.randint(jax.random.fold_in(rng, 1), (pairs,), 0, 1 << 20) % (room + 1)
    sizes = sizes.at[1:1 + 2 * pairs:2].set(donor - shifted).at[2:2 + 2 * pairs:2].set(receiver + shifted)
    return sizes[jax.random.permutation(jax.random.fold_in(rng, 2), count)]


def scatter_about(own_key, extent, width, bound, cuts=(), kind=jnp.bfloat16):
    entries = width * jax.random.normal(own_key, extent, jnp.float32)
    if cuts:
        entries = entries * level_of(own_key, extent, cuts, -0.22, 0.18)
    return jnp.clip(entries, -bound, bound).astype(kind)


def setup_inputs(seed: int = 0) -> dict:
    key_list = jax.random.split(jax.random.key(seed), 6)
    qkv_img = draw_qkv_img(jax.random.fold_in(key_list[5], 71), 0)
    img_seg = jax.vmap(lambda own: jnp.searchsorted(jnp.cumsum(ragged_sizes(own, REQ_G, SEQ_LEN, SEQ_LEN // 2, 2)), jnp.arange(SEQ_LEN), side="right"))(jax.random.split(key_list[1], GROUPS)).reshape((GROUPS, SEQ_LEN)).astype(jnp.int32)
    text_kv = scatter_about(key_list[2], (REQUESTS, 2, TXT, HEADS * HD), 1.0, 6.0, ((0, 32), (3, 16)))
    txt_len = draw_txt_len(jax.random.fold_in(key_list[5], 71), 0)
    req_slot = jax.random.permutation(key_list[4], REQUESTS).astype(jnp.int32)
    return {"qkv_img": qkv_img, "img_seg": img_seg, "text_kv": text_kv, "txt_len": txt_len, "req_slot": req_slot}


big_negative = -1.0e30


def attend_rows(query, keys, values, allowed):
    scale = 1.0 / (query.shape[-1] ** 0.5)
    scores = jnp.dot(query, keys.T, preferred_element_type=jnp.float32) * scale
    scores = jnp.where(allowed, scores, big_negative)
    top = jnp.max(scores, axis=1, keepdims=True)
    weights = jnp.where(allowed, jnp.exp(scores - top), 0.0)
    total = jnp.sum(weights, axis=1, keepdims=True)
    mixed = jnp.dot(weights.astype(jnp.bfloat16), values, preferred_element_type=jnp.float32)
    return (mixed / total).astype(jnp.bfloat16)


def reference(qkv_img, img_seg, text_kv, txt_len, req_slot):
    owner = jnp.zeros((REQUESTS,), jnp.int32).at[req_slot].set(jnp.arange(REQUESTS, dtype=jnp.int32))

    def one_group(g):
        picks = lax.dynamic_slice_in_dim(owner, g * REQ_G, REQ_G)
        text = text_kv[picks]
        lens = txt_len[picks]
        seg = img_seg[g]
        tok = jnp.arange(TXT, dtype=jnp.int32)
        slots = jnp.arange(REQ_G, dtype=jnp.int32)
        text_seg = jnp.where(tok[None, :] < lens[:, None], slots[:, None], -1).reshape(-1)
        key_seg = jnp.concatenate([seg, text_seg])
        allowed = seg[:, None] == key_seg[None, :]
        block = qkv_img[g]

        def one_head(h):
            query = lax.dynamic_slice_in_dim(block[:, 0], h * HD, HD, 1)
            image_keys = lax.dynamic_slice_in_dim(block[:, 1], h * HD, HD, 1)
            image_values = lax.dynamic_slice_in_dim(block[:, 2], h * HD, HD, 1)
            text_keys = lax.dynamic_slice_in_dim(text[:, 0], h * HD, HD, 2).reshape(REQ_G * TXT, HD)
            text_values = lax.dynamic_slice_in_dim(text[:, 1], h * HD, HD, 2).reshape(REQ_G * TXT, HD)
            keys = jnp.concatenate([image_keys, text_keys], 0)
            values = jnp.concatenate([image_values, text_values], 0)
            return attend_rows(query, keys, values, allowed)

        heads = lax.map(one_head, jnp.arange(HEADS, dtype=jnp.int32))
        return jnp.transpose(heads, (1, 0, 2)).reshape(SEQ_LEN, HEADS * HD)

    return lax.map(one_group, jnp.arange(GROUPS, dtype=jnp.int32))
```

```python
import functools

import jax
import jax.numpy as jnp
from jax import lax
from jax.experimental import pallas as pl
from jax.experimental.pallas import tpu as pltpu
from jax.sharding import PartitionSpec as P

HD = 128
REQ_G = 4
GRID = (2, 4, 4)
MESH = pl.DeviceIdType.MESH

FAR = -2097152.0
LOG2E = 1.4426950408889634


def kernel(
    dims,
    slot_ref, len_ref, x_ref, seg_ref, text_ref,
    out_ref,
    kv, k_mask, qb, q_mask, ob, landed, score, prob, seg_send, segs, meta_send, meta_y, meta_sm, text_y, text_xs, text_x, meta_xs, meta_x, meta_xm,
    local_sem, seg_ss, seg_rs, kv_ss, kv_rs, q_ss, q_rs, o_ss, o_rs,
    tz_s, tz_r, ty_s, ty_r, tx_s, tx_r,
):
    n_seq, n_sect, n_hi, n_x, n_y = dims
    blocks = n_seq * n_sect
    tok = x_ref.shape[1]
    img = blocks * tok
    txt = text_ref.shape[2]
    keys = img + REQ_G * txt
    sect, grp, seq = lax.axis_index("sect"), lax.axis_index("grp"), lax.axis_index("seq")
    z_hi, gx, gy = lax.div(grp, n_x * n_y), lax.rem(lax.div(grp, n_y), n_x), lax.rem(grp, n_y)

    def chip_at(d):
        total, unit = 0, 1
        while unit < n_seq:
            total = total + unit * lax.rem(lax.div(seq, unit) + lax.div(d, unit), 2)
            unit *= 2
        return total

    def core_at(c):
        return lax.rem(sect + c, n_sect)

    def columns(d, c):
        return pl.ds(pl.multiple_of((core_at(c) * n_seq + chip_at(d)) * HD, HD), HD)

    def peer(d, c):
        return {"sect": core_at(c), "grp": grp, "seq": chip_at(d)}

    def member(hi, x, y):
        return (hi * n_x + x) * n_y + y

    def peer_group(hi, x, y):
        return {"sect": sect, "grp": member(hi, x, y), "seq": seq}

    def far(k):
        return peer_group(lax.rem(z_hi + k, n_hi), gx, gy)

    def along_y(k):
        return peer_group(z_hi, gx, lax.rem(gy + k, n_y))

    def along_x(k):
        return peer_group(z_hi, lax.rem(gx + k, n_x), gy)

    zero = jnp.int32(0)

    def each_peer(body):
        @pl.loop(1, n_seq)
        def _(i):
            for c in range(n_sect):
                body(n_seq - i, c)

        for c in range(1, n_sect):
            body(zero, c)

    lane = lax.broadcasted_iota(jnp.int32, (8, 128), 1)
    meta = jnp.zeros((8, 128), jnp.int32)
    for r in range(REQ_G):
        meta = jnp.where(lane == r, slot_ref[r], meta)
        meta = jnp.where(lane == REQ_G + r, len_ref[r], meta)
    meta_send[...] = meta
    meta_y[0, 0] = meta
    seg_send[...] = jnp.broadcast_to(seg_ref[...], (8, tok))
    segs[0] = jnp.broadcast_to(seg_ref[...], (8, tok))

    barrier = pltpu.get_barrier_semaphore()

    def greet(device):
        pl.semaphore_signal(barrier, inc=1, device_id=device, device_id_type=MESH)

    each_peer(lambda d, c: greet(peer(d, c)))
    greet(far(1))
    for k in range(1, n_y):
        greet(along_y(k))
    for k in range(1, n_x):
        greet(along_x(k))
    pl.semaphore_wait(barrier, blocks - 1 + 1 + (n_y - 1) + (n_x - 1))

    def remote(src, dst, ss, rs, device):
        return pltpu.make_async_remote_copy(
            src_ref=src, dst_ref=dst, send_sem=ss, recv_sem=rs, device_id=device, device_id_type=MESH)

    def hop_z():
        return (
            remote(meta_send, meta_y.at[0, 1], tz_s.at[0], tz_r.at[0], far(1)),
            remote(text_ref, text_y.at[0, 1], tz_s.at[1], tz_r.at[1], far(1)),
        )

    for copy in hop_z():
        copy.start()

    def move_seg(d, c):
        at = d * n_sect + c
        return remote(seg_send, segs.at[at], seg_ss.at[at], seg_rs.at[at], peer(d, c))

    def move_kv(d, c):
        at = d * n_sect + c
        return remote(x_ref.at[pl.ds(1, 2), :, columns(d, c)], kv.at[at], kv_ss.at[at], kv_rs.at[at], peer(d, c))

    def move_q(d, c):
        at = d * n_sect + c
        return remote(x_ref.at[0, :, columns(d, c)], qb.at[at], q_ss.at[at], q_rs.at[at], peer(d, c))

    def move_o(d, c):
        at = d * n_sect + c
        return remote(ob.at[at], landed.at[at], o_ss.at[at], o_rs.at[at], peer(d, c))

    each_peer(lambda d, c: move_seg(d, c).start())
    each_peer(lambda d, c: move_kv(d, c).start())

    own_text = pltpu.make_async_copy(text_ref, text_y.at[0, 0], local_sem.at[0])
    own_text.start()
    own_kv = pltpu.make_async_copy(x_ref.at[pl.ds(1, 2), :, columns(zero, 0)], kv.at[0], local_sem.at[1])
    own_kv.start()
    own_q = pltpu.make_async_copy(x_ref.at[0, :, columns(zero, 0)], qb.at[0], local_sem.at[2])
    own_q.start()
    each_peer(lambda d, c: move_q(d, c).start())

    each_peer(lambda d, c: move_seg(d, c).wait())

    spot = lax.broadcasted_iota(jnp.int32, (tok, HD), 1)

    @pl.loop(0, blocks)
    def _(b):
        row = segs[b]
        across = jnp.broadcast_to(row[0:1, :], (tok, tok))
        down = jnp.transpose(across)
        q_mask[b] = jnp.where(spot == down, 1.0, 0.0).astype(jnp.bfloat16)
        k_mask[b] = jnp.where((spot < REQ_G) & (spot != down), FAR, 0.0).astype(jnp.bfloat16)

    own_text.wait()
    for copy in hop_z():
        copy.wait()

    def hop_y(k):
        return (
            remote(meta_y.at[0], meta_y.at[k], ty_s.at[0, k], ty_r.at[0, k], along_y(k)),
            remote(text_y.at[0], text_y.at[k], ty_s.at[1, k], ty_r.at[1, k], along_y(k)),
        )

    for k in range(1, n_y):
        for copy in hop_y(k):
            copy.start()
    for k in range(1, n_y):
        for copy in hop_y(k):
            copy.wait()

    to_scalars = pltpu.make_async_copy(meta_y, meta_sm, local_sem.at[3])
    to_scalars.start()
    to_scalars.wait()

    for k in range(n_x):
        first = member(z_hi, lax.rem(gx + k, n_x), gy) * REQ_G
        lens = jnp.zeros((8, 128), jnp.int32)
        for j in range(REQ_G):
            def look(s, carry):
                at_y, at_hi, at_r, count = carry
                sy, sh, sr = lax.div(s, n_hi * REQ_G), lax.rem(lax.div(s, REQ_G), n_hi), lax.rem(s, REQ_G)
                hit = meta_sm[sy, sh, 0, sr] == first + j
                return (
                    jnp.where(hit, sy, at_y),
                    jnp.where(hit, sh, at_hi),
                    jnp.where(hit, sr, at_r),
                    jnp.where(hit, meta_sm[sy, sh, 0, REQ_G + sr], count),
                )

            at_y, at_hi, at_r, count = lax.fori_loop(0, n_y * n_hi * REQ_G, look, (zero, zero, zero, zero))
            text_xs[k, j] = text_y[at_y, at_hi, at_r]
            lens = jnp.where(lane == j, count, lens)
        meta_xs[k] = lens

    def hop_x(k):
        return (
            remote(meta_xs.at[k], meta_x.at[k], tx_s.at[0, k], tx_r.at[0, k], along_x(k)),
            remote(text_xs.at[k], text_x.at[k], tx_s.at[1, k], tx_r.at[1, k], along_x(k)),
        )

    for k in range(1, n_x):
        for copy in hop_x(k):
            copy.start()
    for k in range(1, n_x):
        for copy in hop_x(k):
            copy.wait()
    text_x[0] = text_xs[0]
    meta_x[0] = meta_xs[0]

    to_scalars = pltpu.make_async_copy(meta_x, meta_xm, local_sem.at[4])
    to_scalars.start()
    to_scalars.wait()

    own_kv.wait()
    own_q.wait()
    each_peer(lambda d, c: move_kv(d, c).wait())

    place = lax.broadcasted_iota(jnp.int32, (txt, HD), 0)
    spot_t = lax.broadcasted_iota(jnp.int32, (txt, HD), 1)
    for j in range(REQ_G):
        at_x, count = zero, zero
        for k in range(n_x):
            here = meta_xm[k, 0, j]
            at_x = jnp.where(here > 0, k, at_x)
            count = jnp.where(here > 0, here, count)
        block, part = blocks + (j * txt) // tok, pl.ds((j * txt) % tok, txt)
        kv[block, 0, part] = text_x[at_x, j, 0]
        kv[block, 1, part] = text_x[at_x, j, 1]
        live = (spot_t == j) & (place < count)
        k_mask[block, part] = jnp.where((spot_t < REQ_G) & ~live, FAR, 0.0).astype(jnp.bfloat16)

    factor = LOG2E / HD ** 0.5
    pair = n_sect * tok

    def attend(d):
        both = pl.ds(d * n_sect, n_sect)
        score[...] = lax.dot_general(
            jnp.concatenate([qb[both].reshape(pair, HD), q_mask[both].reshape(pair, HD)], axis=1),
            jnp.concatenate([kv[:, 0].reshape(keys, HD), k_mask[...].reshape(keys, HD)], axis=1),
            (((1,), (1,)), ((), ())), preferred_element_type=jnp.float32)
        top = jnp.max(score[...], axis=1, keepdims=True)
        prob[...] = jnp.exp2((score[...] - top) * factor).astype(jnp.bfloat16)
        mixed = jnp.dot(
            prob[...], jnp.concatenate([kv[:, 1].reshape(keys, HD), jnp.ones((keys, HD), jnp.bfloat16)], axis=1),
            preferred_element_type=jnp.float32)
        ob[both] = (mixed[:, :HD] / mixed[:, HD:]).astype(jnp.bfloat16).reshape(n_sect, tok, HD)

    for c in range(1, n_sect):
        move_q(zero, c).wait()
    attend(0)
    for c in range(1, n_sect):
        move_o(zero, c).start()

    @pl.loop(1, n_seq)
    def _(i):
        d = n_seq - i
        for c in range(n_sect):
            move_q(d, c).wait()
        attend(d)
        for c in range(n_sect):
            move_o(d, c).start()

    out_ref[:, columns(zero, 0)] = ob[0]

    def finish(d, c):
        move_o(d, c).wait()
        out_ref[:, columns(d, c)] = landed[d * n_sect + c]

    each_peer(finish)


def local(mesh, qkv_img, img_seg, text_kv, txt_len, req_slot):
    n_seq, n_sect = mesh.shape["seq"], mesh.shape["sect"]
    n_hi, n_x, n_y = GRID
    blocks = n_seq * n_sect
    tok, width = qkv_img.shape[1], qkv_img.shape[3]
    txt = text_kv.shape[2]
    keys = blocks * tok + REQ_G * txt
    x = jnp.transpose(qkv_img[0], (1, 0, 2))
    dma = pltpu.SemaphoreType.DMA
    bf16, i32 = jnp.bfloat16, jnp.int32
    out = pl.pallas_call(
        functools.partial(kernel, (n_seq, n_sect, n_hi, n_x, n_y)),
        out_shape=jax.ShapeDtypeStruct((tok, width), bf16),
        in_specs=[
            pl.BlockSpec(memory_space=pltpu.SMEM),
            pl.BlockSpec(memory_space=pltpu.SMEM),
            pl.BlockSpec(memory_space=pl.ANY),
            pl.BlockSpec(memory_space=pltpu.VMEM),
            pl.BlockSpec(memory_space=pl.ANY),
        ],
        out_specs=pl.BlockSpec(memory_space=pltpu.VMEM),
        scratch_shapes=[
            pltpu.VMEM((keys // tok, 2, tok, HD), bf16),
            pltpu.VMEM((keys // tok, tok, HD), bf16),
            pltpu.VMEM((blocks, tok, HD), bf16),
            pltpu.VMEM((blocks, tok, HD), bf16),
            pltpu.VMEM((blocks, tok, HD), bf16),
            pltpu.VMEM((blocks, tok, HD), bf16),
            pltpu.VMEM((n_sect * tok, keys), jnp.float32),
            pltpu.VMEM((n_sect * tok, keys), bf16),
            pltpu.VMEM((8, tok), i32),
            pltpu.VMEM((blocks, 8, tok), i32),
            pltpu.VMEM((8, 128), i32),
            pltpu.VMEM((n_y, n_hi, 8, 128), i32),
            pltpu.SMEM((n_y, n_hi, 8, 128), i32),
            pltpu.VMEM((n_y, n_hi, REQ_G, 2, txt, HD), bf16),
            pltpu.VMEM((n_x, REQ_G, 2, txt, HD), bf16),
            pltpu.VMEM((n_x, REQ_G, 2, txt, HD), bf16),
            pltpu.VMEM((n_x, 8, 128), i32),
            pltpu.VMEM((n_x, 8, 128), i32),
            pltpu.SMEM((n_x, 8, 128), i32),
            dma((5,)),
            dma((blocks,)), dma((blocks,)),
            dma((blocks,)), dma((blocks,)),
            dma((blocks,)), dma((blocks,)),
            dma((blocks,)), dma((blocks,)),
            dma((2,)), dma((2,)),
            dma((2, n_y)), dma((2, n_y)),
            dma((2, n_x)), dma((2, n_x)),
        ],
        compiler_params=pltpu.CompilerParams(
            collective_id=0, has_side_effects=True, vmem_limit_bytes=40 * 1024 * 1024),
        name="routed_attention",
    )(req_slot, txt_len, x, img_seg, text_kv)
    return out[None]


def solution(mesh):
    return jax.shard_map(
        functools.partial(local, mesh),
        mesh=mesh,
        in_specs=(
            P("grp", ("sect", "seq"), None, None),
            P("grp", ("sect", "seq")),
            P("grp", None, None, ("sect", "seq")),
            P("grp"),
            P("grp"),
        ),
        out_specs=P("grp", ("sect", "seq"), None),
        check_vma=False,
    )
```

```python
import functools

import jax
import jax.numpy as jnp
from jax import lax
from jax.experimental import pallas as pl
from jax.experimental.pallas import tpu as pltpu
from jax.sharding import PartitionSpec as P

HD = 128
REQ_G = 4
GRID = (2, 4, 4)
MESH = pl.DeviceIdType.MESH

FAR = -2097152.0
LOG2E = 1.4426950408889634


def kernel(
    dims,
    slot_ref, len_ref, x_ref, seg_ref, text_ref,
    out_ref,
    kv, k_mask, qb, q_mask, ob, landed, score, prob, seg_send, segs,
    text_in, text_y, text_xs, text_x, text_far, text_own,
    meta_send, meta_in, meta_y, picks, meta_xs, meta_x, meta_far, meta_own,
    meta_sm, picks_sm, meta_xm, meta_own_sm, slots, counts, seg_row,
    local_sem, seg_ss, seg_rs, kv_ss, kv_rs, q_ss, q_rs, o_ss, o_rs,
    ta_s, ta_r, tb_s, tb_r, ty_s, ty_r, tx_s, tx_r, tc_s, tc_r,
):
    n_seq, n_sect, n_hi, n_x, n_y = dims
    blocks = n_seq * n_sect
    tok = x_ref.shape[1]
    img = blocks * tok
    txt = text_ref.shape[2]
    keys = img + REQ_G * txt
    sect, grp, seq = lax.axis_index("sect"), lax.axis_index("grp"), lax.axis_index("seq")
    z_hi, gx, gy = lax.div(grp, n_x * n_y), lax.rem(lax.div(grp, n_y), n_x), lax.rem(grp, n_y)

    def chip_at(d):
        total, unit = 0, 1
        while unit < n_seq:
            bit = (d // unit) % 2 if isinstance(d, int) else lax.div(d, unit)
            total = total + unit * lax.rem(lax.div(seq, unit) + bit, 2)
            unit *= 2
        return total

    def core_at(c):
        return lax.rem(sect + c, n_sect)

    def columns(d, c):
        chip = chip_at(d)
        head = core_at(c) * n_seq + chip + z_hi * (n_seq - 1 - 2 * chip)
        return pl.ds(pl.multiple_of(head * HD, HD), HD)

    def peer(d, c):
        return {"sect": core_at(c), "grp": grp, "seq": chip_at(d)}

    def member(hi, x, y):
        return (hi * n_x + x) * n_y + y

    far = {"sect": sect, "grp": member(n_hi - 1 - z_hi, gx, gy), "seq": n_seq - 1 - seq}

    def along_y(k):
        return {"sect": sect, "grp": member(z_hi, gx, lax.rem(gy + k, n_y)), "seq": seq}

    def along_x(k):
        return {"sect": sect, "grp": member(z_hi, lax.rem(gx + k, n_x), gy), "seq": seq}

    lower, upper = z_hi == 0, z_hi == 1

    def nth(i):
        return n_seq // 2 + (2 * (i % 2) - 1) * (i // 2) if isinstance(i, int) else (
            n_seq // 2 + (2 * lax.rem(i, 2) - 1) * lax.div(i, 2))

    order = [(nth(i), c) for i in range(1, n_seq) for c in range(n_sect)] + [(0, c) for c in range(1, n_sect)]

    def some(places, body):
        for d, c in places:
            body(d, c)

    def each_peer(body):
        @pl.loop(1, n_seq)
        def _(i):
            for c in range(n_sect):
                body(nth(i), c)

        for c in range(1, n_sect):
            body(0, c)

    small = (
        pltpu.make_async_copy(slot_ref, slots, local_sem.at[5]),
        pltpu.make_async_copy(len_ref, counts, local_sem.at[6]),
        pltpu.make_async_copy(seg_ref, seg_row, local_sem.at[7]),
    )
    for copy in small:
        copy.start()

    barrier = pltpu.get_barrier_semaphore()

    def greet(device):
        pl.semaphore_signal(barrier, inc=1, device_id=device, device_id_type=MESH)

    each_peer(lambda d, c: greet(peer(d, c)))

    @pl.when(lower)
    def _():
        for k in range(1, n_y):
            greet(along_y(k))
        for k in range(1, n_x):
            greet(along_x(k))

    for copy in small:
        copy.wait()
    lane = lax.broadcasted_iota(jnp.int32, (8, 128), 1)
    meta = jnp.zeros((8, 128), jnp.int32)
    for r in range(REQ_G):
        meta = jnp.where(lane == r, slots[r], meta)
        meta = jnp.where(lane == REQ_G + r, counts[r], meta)
    meta_send[...] = meta
    seg_send[...] = jnp.broadcast_to(seg_row[...], (8, tok))
    segs[0] = jnp.broadcast_to(seg_row[...], (8, tok))

    @pl.when(lower)
    def _():
        pl.semaphore_wait(barrier, blocks - 1 + n_y - 1 + n_x - 1)
        greet(far)

    @pl.when(upper)
    def _():
        pl.semaphore_wait(barrier, blocks - 1 + 1)
        greet(far)

    def remote(src, dst, ss, rs, device):
        return pltpu.make_async_remote_copy(
            src_ref=src, dst_ref=dst, send_sem=ss, recv_sem=rs, device_id=device, device_id_type=MESH)

    def start(copies):
        for copy in copies:
            copy.start()

    def wait(copies):
        for copy in copies:
            copy.wait()

    def hop_mirror():
        mate = peer(n_seq - 1, 0)
        return (
            remote(meta_send, meta_in, ta_s.at[0], ta_r.at[0], mate),
            remote(text_ref, text_in, ta_s.at[1], ta_r.at[1], mate),
        )

    def requests(half, k):
        return pl.ds((half * n_y + k) * REQ_G, REQ_G)

    def hop_down():
        return (
            remote(meta_in, meta_y.at[n_y], tb_s.at[0], tb_r.at[0], far),
            remote(text_in, text_y.at[requests(1, 0)], tb_s.at[1], tb_r.at[1], far),
        )

    def hop_y(half, k):
        meta_src = meta_y.at[n_y] if half else meta_send
        text_src = text_y.at[requests(1, 0)] if half else text_ref
        return (
            remote(meta_src, meta_y.at[half * n_y + k], ty_s.at[0, half, k], ty_r.at[0, half, k], along_y(k)),
            remote(text_src, text_y.at[requests(half, k)], ty_s.at[1, half, k], ty_r.at[1, half, k], along_y(k)),
        )

    def hop_x(k):
        return (
            remote(meta_xs, meta_x.at[k], tx_s.at[0, k], tx_r.at[0, k], along_x(k)),
            remote(text_xs.at[k], text_x.at[k], tx_s.at[1, k], tx_r.at[1, k], along_x(k)),
        )

    def hop_up():
        return (
            remote(meta_far, meta_own, tc_s.at[0], tc_r.at[0], far),
            remote(text_far, text_own, tc_s.at[1], tc_r.at[1], far),
        )

    def move_seg(d, c):
        at = d * n_sect + c
        return remote(seg_send, segs.at[at], seg_ss.at[at], seg_rs.at[at], peer(d, c))

    def move_kv(d, c):
        at = d * n_sect + c
        return remote(x_ref.at[pl.ds(1, 2), :, columns(d, c)], kv.at[at], kv_ss.at[at], kv_rs.at[at], peer(d, c))

    def move_q(d, c):
        at = d * n_sect + c
        return remote(x_ref.at[0, :, columns(d, c)], qb.at[at], q_ss.at[at], q_rs.at[at], peer(d, c))

    def move_o(d, c):
        at = d * n_sect + c
        return remote(ob.at[at], landed.at[at], o_ss.at[at], o_rs.at[at], peer(d, c))

    def send_kv(d, c):
        move_kv(d, c).start()

    def send_q(d, c):
        move_q(d, c).start()

    n1, n2 = 2 * n_sect, 5 * n_sect

    @pl.when(upper)
    def _():
        start(hop_mirror())

    each_peer(lambda d, c: move_seg(d, c).start())

    @pl.when(lower)
    def _():
        for k in range(1, n_y):
            start(hop_y(0, k))

    some(order[:n1], send_kv)

    own_text = pltpu.make_async_copy(text_ref, text_y.at[requests(0, 0)], local_sem.at[0])
    own_text.start()
    own_kv = pltpu.make_async_copy(x_ref.at[pl.ds(1, 2), :, columns(0, 0)], kv.at[0], local_sem.at[1])
    own_kv.start()
    own_q = pltpu.make_async_copy(x_ref.at[0, :, columns(0, 0)], qb.at[0], local_sem.at[2])
    own_q.start()
    meta_y[0] = meta

    @pl.when(upper)
    def _():
        wait(hop_mirror())
        start(hop_down())

    some(order[n1:n2], send_kv)

    each_peer(lambda d, c: move_seg(d, c).wait())

    spot = lax.broadcasted_iota(jnp.int32, (tok, HD), 1)

    @pl.loop(0, blocks)
    def _(b):
        row = segs[b]
        across = jnp.broadcast_to(row[0:1, :], (tok, tok))
        down = jnp.transpose(across)
        q_mask[b] = jnp.where(spot == down, 1.0, 0.0).astype(jnp.bfloat16)
        k_mask[b] = jnp.where((spot < REQ_G) & (spot != down), FAR, 0.0).astype(jnp.bfloat16)

    @pl.when(lower)
    def _():
        for copy in hop_down():
            copy.wait_recv()
        for k in range(1, n_y):
            start(hop_y(1, k))

    @pl.when(upper)
    def _():
        for copy in hop_down():
            copy.wait_send()

    some(order[n2:], send_kv)
    own_text.wait()

    @pl.when(lower)
    def _():
        for half in range(n_hi):
            for k in range(1, n_y):
                wait(hop_y(half, k))
        to_scalars = pltpu.make_async_copy(meta_y, meta_sm, local_sem.at[3])
        to_scalars.start()
        to_scalars.wait()
        per_x = n_hi * REQ_G
        to_x = lax.rem(gx + lax.div(lane, per_x), n_x)
        to_hi = lax.rem(lax.div(lane, REQ_G), n_hi)
        wanted = member(to_hi, to_x, gy) * REQ_G + lax.rem(lane, REQ_G)
        wanted = jnp.where(lane < n_x * per_x, wanted, -1)
        at, lens = jnp.zeros((8, 128), jnp.int32), jnp.zeros((8, 128), jnp.int32)
        for b in range(n_hi * n_y):
            for r in range(REQ_G):
                hit = wanted == meta_sm[b, 0, r]
                at = jnp.where(hit, b * REQ_G + r, at)
                lens = jnp.where(hit, meta_sm[b, 0, REQ_G + r], lens)
        picks[...] = at
        meta_xs[...] = lens
        to_scalars = pltpu.make_async_copy(picks, picks_sm, local_sem.at[3])
        to_scalars.start()
        to_scalars.wait()
        for k in range(n_x):
            for j in range(per_x):
                text_xs[k, j] = text_y[picks_sm[0, k * per_x + j]]
        for k in range(1, n_x):
            start(hop_x(k))

    some(order[:4 * n_sect], send_q)

    @pl.when(lower)
    def _():
        for k in range(1, n_x):
            wait(hop_x(k))
        text_x[0] = text_xs[0]
        meta_x[0] = meta_xs[...]
        to_scalars = pltpu.make_async_copy(meta_x, meta_xm, local_sem.at[3])
        to_scalars.start()
        to_scalars.wait()
        for half, (text_to, meta_to) in enumerate(((text_own, meta_own), (text_far, meta_far))):
            lens = jnp.zeros((8, 128), jnp.int32)
            for j in range(REQ_G):
                at_x, count = jnp.int32(0), jnp.int32(0)
                for k in range(n_x):
                    here = meta_xm[k, 0, (k * n_hi + half) * REQ_G + j]
                    at_x = jnp.where(here > 0, k, at_x)
                    count = jnp.where(here > 0, here, count)
                text_to[j] = text_x[at_x, half * REQ_G + j]
                lens = jnp.where(lane == j, count, lens)
            meta_to[...] = lens
        pl.semaphore_wait(barrier, 1)
        start(hop_up())

    some(order[4 * n_sect:], send_q)

    @pl.when(upper)
    def _():
        for copy in hop_up():
            copy.wait_recv()

    to_scalars = pltpu.make_async_copy(meta_own, meta_own_sm, local_sem.at[4])
    to_scalars.start()
    to_scalars.wait()

    place = lax.broadcasted_iota(jnp.int32, (txt, HD), 0)
    spot_t = lax.broadcasted_iota(jnp.int32, (txt, HD), 1)
    for j in range(REQ_G):
        block, part = blocks + (j * txt) // tok, pl.ds((j * txt) % tok, txt)
        kv[block, 0, part] = text_own[j, 0]
        kv[block, 1, part] = text_own[j, 1]
        live = (spot_t == j) & (place < meta_own_sm[0, j])
        k_mask[block, part] = jnp.where((spot_t < REQ_G) & ~live, FAR, 0.0).astype(jnp.bfloat16)

    own_kv.wait()
    own_q.wait()
    each_peer(lambda d, c: move_kv(d, c).wait())

    factor = LOG2E / HD ** 0.5
    pair = n_sect * tok

    def attend(d):
        both = pl.ds(d * n_sect, n_sect)
        score[...] = lax.dot_general(
            jnp.concatenate([qb[both].reshape(pair, HD), q_mask[both].reshape(pair, HD)], axis=1),
            jnp.concatenate([kv[:, 0].reshape(keys, HD), k_mask[...].reshape(keys, HD)], axis=1),
            (((1,), (1,)), ((), ())), preferred_element_type=jnp.float32)
        top = jnp.max(score[...], axis=1, keepdims=True)
        prob[...] = jnp.exp2((score[...] - top) * factor).astype(jnp.bfloat16)
        mixed = jnp.dot(
            prob[...], jnp.concatenate([kv[:, 1].reshape(keys, HD), jnp.ones((keys, HD), jnp.bfloat16)], axis=1),
            preferred_element_type=jnp.float32)
        ob[both] = (mixed[:, :HD] / mixed[:, HD:]).astype(jnp.bfloat16).reshape(n_sect, tok, HD)

    for c in range(1, n_sect):
        move_q(0, c).wait()
    attend(0)
    for c in range(1, n_sect):
        move_o(0, c).start()

    @pl.loop(1, n_seq)
    def _(i):
        d = nth(i)
        for c in range(n_sect):
            move_q(d, c).wait()
        attend(d)
        for c in range(n_sect):
            move_o(d, c).start()

    @pl.when(lower)
    def _():
        for copy in hop_up():
            copy.wait_send()

    out_ref[:, columns(0, 0)] = ob[0]

    def finish(d, c):
        move_o(d, c).wait()
        out_ref[:, columns(d, c)] = landed[d * n_sect + c]

    each_peer(finish)


def local(mesh, qkv_img, img_seg, text_kv, txt_len, req_slot):
    n_seq, n_sect = mesh.shape["seq"], mesh.shape["sect"]
    n_hi, n_x, n_y = GRID
    blocks = n_seq * n_sect
    tok, width = qkv_img.shape[1], qkv_img.shape[3]
    txt = text_kv.shape[2]
    keys = blocks * tok + REQ_G * txt
    x = jnp.transpose(qkv_img[0], (1, 0, 2))
    dma = pltpu.SemaphoreType.DMA
    bf16, i32 = jnp.bfloat16, jnp.int32
    out = pl.pallas_call(
        functools.partial(kernel, (n_seq, n_sect, n_hi, n_x, n_y)),
        out_shape=jax.ShapeDtypeStruct((tok, width), bf16),
        in_specs=[
            pl.BlockSpec(memory_space=pl.ANY),
            pl.BlockSpec(memory_space=pl.ANY),
            pl.BlockSpec(memory_space=pl.ANY),
            pl.BlockSpec(memory_space=pl.ANY),
            pl.BlockSpec(memory_space=pl.ANY),
        ],
        out_specs=pl.BlockSpec(memory_space=pltpu.VMEM),
        scratch_shapes=[
            pltpu.VMEM((keys // tok, 2, tok, HD), bf16),
            pltpu.VMEM((keys // tok, tok, HD), bf16),
            pltpu.VMEM((blocks, tok, HD), bf16),
            pltpu.VMEM((blocks, tok, HD), bf16),
            pltpu.VMEM((blocks, tok, HD), bf16),
            pltpu.VMEM((blocks, tok, HD), bf16),
            pltpu.VMEM((n_sect * tok, keys), jnp.float32),
            pltpu.VMEM((n_sect * tok, keys), bf16),
            pltpu.VMEM((8, tok), i32),
            pltpu.VMEM((blocks, 8, tok), i32),
            pltpu.VMEM((REQ_G, 2, txt, HD), bf16),
            pltpu.VMEM((n_hi * n_y * REQ_G, 2, txt, HD), bf16),
            pltpu.VMEM((n_x, n_hi * REQ_G, 2, txt, HD), bf16),
            pltpu.VMEM((n_x, n_hi * REQ_G, 2, txt, HD), bf16),
            pltpu.VMEM((REQ_G, 2, txt, HD), bf16),
            pltpu.VMEM((REQ_G, 2, txt, HD), bf16),
            pltpu.VMEM((8, 128), i32),
            pltpu.VMEM((8, 128), i32),
            pltpu.VMEM((n_hi * n_y, 8, 128), i32),
            pltpu.VMEM((8, 128), i32),
            pltpu.VMEM((8, 128), i32),
            pltpu.VMEM((n_x, 8, 128), i32),
            pltpu.VMEM((8, 128), i32),
            pltpu.VMEM((8, 128), i32),
            pltpu.SMEM((n_hi * n_y, 8, 128), i32),
            pltpu.SMEM((8, 128), i32),
            pltpu.SMEM((n_x, 8, 128), i32),
            pltpu.SMEM((8, 128), i32),
            pltpu.SMEM((REQ_G,), i32),
            pltpu.SMEM((REQ_G,), i32),
            pltpu.VMEM((1, tok), i32),
            dma((8,)),
            dma((blocks,)), dma((blocks,)),
            dma((blocks,)), dma((blocks,)),
            dma((blocks,)), dma((blocks,)),
            dma((blocks,)), dma((blocks,)),
            dma((2,)), dma((2,)),
            dma((2,)), dma((2,)),
            dma((2, n_hi, n_y)), dma((2, n_hi, n_y)),
            dma((2, n_x)), dma((2, n_x)),
            dma((2,)), dma((2,)),
        ],
        compiler_params=pltpu.CompilerParams(
            collective_id=0, has_side_effects=True, vmem_limit_bytes=63 * 1024 * 1024),
        name="routed_attention",
    )(req_slot, txt_len, x, img_seg, text_kv)
    return out[None]


def solution(mesh):
    return jax.shard_map(
        functools.partial(local, mesh),
        mesh=mesh,
        in_specs=(
            P("grp", ("sect", "seq"), None, None),
            P("grp", ("sect", "seq")),
            P("grp", None, None, ("sect", "seq")),
            P("grp"),
            P("grp"),
        ),
        out_specs=P("grp", ("sect", "seq"), None),
        check_vma=False,
    )
```

```python
import functools

import jax
import jax.numpy as jnp
from jax import lax
from jax.experimental import pallas as pl
from jax.experimental.pallas import tpu as pltpu
from jax.sharding import PartitionSpec as P

HD = 128
REQ_G = 4
GRID = (2, 4, 4)
SPLIT = 3
MESH = pl.DeviceIdType.MESH

FAR = -2097152.0
LOG2E = 1.4426950408889634


def kernel(
    dims,
    slot_ref, len_ref, x_ref, seg_ref, text_ref,
    out_ref,
    kv, k_mask, qb, q_mask, ob, landed, score, prob, seg_send, segs,
    text_in, text_y, text_xs, text_x, text_far, text_own,
    meta_send, meta_in, meta_y, picks, meta_xs, meta_x, meta_far, meta_own,
    meta_sm, picks_sm, meta_xm, meta_own_sm, slots, counts, seg_row,
    local_sem, far_in, seg_ss, seg_rs, kv_ss, kv_rs, q_ss, q_rs, o_ss, o_rs,
    ta_s, ta_r, tb_s, tb_r, td_s, td_r, ty_s, ty_r, tx_s, tx_r, tc_s, tc_r,
):
    n_seq, n_sect, n_hi, n_x, n_y = dims
    blocks = n_seq * n_sect
    tok = x_ref.shape[1]
    img = blocks * tok
    txt = text_ref.shape[2]
    keys = img + REQ_G * txt
    sect, grp, seq = lax.axis_index("sect"), lax.axis_index("grp"), lax.axis_index("seq")
    z_hi, gx, gy = lax.div(grp, n_x * n_y), lax.rem(lax.div(grp, n_y), n_x), lax.rem(grp, n_y)

    def chip_at(d):
        total, unit = 0, 1
        while unit < n_seq:
            bit = (d // unit) % 2 if isinstance(d, int) else lax.div(d, unit)
            total = total + unit * lax.rem(lax.div(seq, unit) + bit, 2)
            unit *= 2
        return total

    def core_at(c):
        return lax.rem(sect + c, n_sect)

    def columns(d, c):
        chip = chip_at(d)
        head = core_at(c) * n_seq + chip + z_hi * (n_seq - 1 - 2 * chip)
        return pl.ds(pl.multiple_of(head * HD, HD), HD)

    def peer(d, c):
        return {"sect": core_at(c), "grp": grp, "seq": chip_at(d)}

    def member(hi, x, y):
        return (hi * n_x + x) * n_y + y

    far = {"sect": sect, "grp": member(n_hi - 1 - z_hi, gx, gy), "seq": n_seq - 1 - seq}

    def along_y(k):
        return {"sect": sect, "grp": member(z_hi, gx, lax.rem(gy + k, n_y)), "seq": seq}

    def along_x(k):
        return {"sect": sect, "grp": member(z_hi, lax.rem(gx + k, n_x), gy), "seq": seq}

    lower, upper = z_hi == 0, z_hi == 1

    def nth(i):
        return n_seq // 2 + (2 * (i % 2) - 1) * (i // 2) if isinstance(i, int) else (
            n_seq // 2 + (2 * lax.rem(i, 2) - 1) * lax.div(i, 2))

    order = [(d, c) for a, b in ((4, 3), (5, 2), (6, 1)) for c in range(n_sect) for d in (a, b)] + [(7, 0), (7, 1)] + [(0, c) for c in range(1, n_sect)]

    def some(places, body):
        for d, c in places:
            body(d, c)

    def each_peer(body):
        @pl.loop(1, n_seq)
        def _(i):
            for c in range(n_sect):
                body(nth(i), c)

        for c in range(1, n_sect):
            body(0, c)

    small = (
        pltpu.make_async_copy(slot_ref, slots, local_sem.at[5]),
        pltpu.make_async_copy(len_ref, counts, local_sem.at[6]),
        pltpu.make_async_copy(seg_ref, seg_row, local_sem.at[7]),
    )
    for copy in small:
        copy.start()

    barrier = pltpu.get_barrier_semaphore()

    def greet(device):
        pl.semaphore_signal(barrier, inc=1, device_id=device, device_id_type=MESH)

    each_peer(lambda d, c: greet(peer(d, c)))

    @pl.when(lower)
    def _():
        for k in range(1, n_y):
            greet(along_y(k))
        for k in range(1, n_x):
            greet(along_x(k))
        greet(far)

    for copy in small:
        copy.wait()
    lane = lax.broadcasted_iota(jnp.int32, (8, 128), 1)
    meta = jnp.zeros((8, 128), jnp.int32)
    for r in range(REQ_G):
        meta = jnp.where(lane == r, slots[r], meta)
        meta = jnp.where(lane == REQ_G + r, counts[r], meta)
    meta_send[...] = meta
    seg_send[...] = jnp.broadcast_to(seg_row[...], (8, tok))
    segs[0] = jnp.broadcast_to(seg_row[...], (8, tok))

    @pl.when(lower)
    def _():
        pl.semaphore_wait(barrier, blocks - 1 + n_y - 1 + n_x - 1)

    @pl.when(upper)
    def _():
        pl.semaphore_wait(barrier, blocks - 1 + 1)
        pl.semaphore_signal(far_in, inc=1, device_id=far, device_id_type=MESH)

    def remote(src, dst, ss, rs, device):
        return pltpu.make_async_remote_copy(
            src_ref=src, dst_ref=dst, send_sem=ss, recv_sem=rs, device_id=device, device_id_type=MESH)

    def start(copies):
        for copy in copies:
            copy.start()

    def wait(copies):
        for copy in copies:
            copy.wait()

    def hop_mirror():
        mate = peer(n_seq - 1, 0)
        return (
            remote(meta_send, meta_in, ta_s.at[0], ta_r.at[0], mate),
            remote(
                text_ref.at[pl.ds(0, SPLIT)], text_in.at[pl.ds(0, SPLIT)],
                ta_s.at[1], ta_r.at[1], mate),
        )

    def requests(half, k):
        return pl.ds((half * n_y + k) * REQ_G, REQ_G)

    def hop_down():
        return (
            remote(meta_in, meta_y.at[n_y], tb_s.at[0], tb_r.at[0], far),
            remote(
                text_in.at[pl.ds(0, SPLIT)], text_y.at[pl.ds(n_y * REQ_G, SPLIT)],
                tb_s.at[1], tb_r.at[1], far),
        )

    late = pl.ds(SPLIT, REQ_G - SPLIT)

    def hop_down_first():
        return remote(text_ref.at[late], text_in.at[late], td_s.at[0], td_r.at[0], far)

    def hop_mirror_last():
        return remote(
            text_in.at[late], text_y.at[pl.ds(n_y * REQ_G + SPLIT, REQ_G - SPLIT)],
            td_s.at[1], td_r.at[1], peer(n_seq - 1, 0))

    def hop_y(half, k):
        meta_src = meta_y.at[n_y] if half else meta_send
        text_src = text_y.at[requests(1, 0)] if half else text_ref
        return (
            remote(meta_src, meta_y.at[half * n_y + k], ty_s.at[0, half, k], ty_r.at[0, half, k], along_y(k)),
            remote(text_src, text_y.at[requests(half, k)], ty_s.at[1, half, k], ty_r.at[1, half, k], along_y(k)),
        )

    def hop_x(k):
        return (
            remote(meta_xs, meta_x.at[k], tx_s.at[0, k], tx_r.at[0, k], along_x(k)),
            remote(text_xs.at[k], text_x.at[k], tx_s.at[1, k], tx_r.at[1, k], along_x(k)),
        )

    def hop_up():
        return (
            remote(meta_far, meta_own, tc_s.at[0], tc_r.at[0], far),
            remote(text_far, text_own, tc_s.at[1], tc_r.at[1], far),
        )

    def move_seg(d, c):
        at = d * n_sect + c
        return remote(seg_send, segs.at[at], seg_ss.at[at], seg_rs.at[at], peer(d, c))

    def move_kv(d, c):
        at = d * n_sect + c
        return remote(x_ref.at[pl.ds(1, 2), :, columns(d, c)], kv.at[at], kv_ss.at[at], kv_rs.at[at], peer(d, c))

    def move_q(d, c):
        at = d * n_sect + c
        return remote(x_ref.at[0, :, columns(d, c)], qb.at[at], q_ss.at[at], q_rs.at[at], peer(d, c))

    def move_o(d, c):
        at = d * n_sect + c
        return remote(ob.at[at], landed.at[at], o_ss.at[at], o_rs.at[at], peer(d, c))

    def send_kv(d, c):
        move_kv(d, c).start()

    def send_q(d, c):
        move_q(d, c).start()

    n1, n2 = 2 * n_sect, 5 * n_sect

    @pl.when(upper)
    def _():
        start(hop_mirror())
        hop_down_first().start()

    some(order[:n_sect], send_kv)
    each_peer(lambda d, c: move_seg(d, c).start())
    some(order[n_sect:n1], send_kv)

    @pl.when(lower)
    def _():
        for k in range(1, n_y):
            start(hop_y(0, k))

    own_text = pltpu.make_async_copy(text_ref, text_y.at[requests(0, 0)], local_sem.at[0])
    own_text.start()
    own_kv = pltpu.make_async_copy(x_ref.at[pl.ds(1, 2), :, columns(0, 0)], kv.at[0], local_sem.at[1])
    own_kv.start()
    own_q = pltpu.make_async_copy(x_ref.at[0, :, columns(0, 0)], qb.at[0], local_sem.at[2])
    own_q.start()
    meta_y[0] = meta

    @pl.when(upper)
    def _():
        wait(hop_mirror())
        start(hop_down())
        hop_down_first().wait_send()

    @pl.when(lower)
    def _():
        hop_down_first().wait_recv()
        hop_mirror_last().start()

    some(order[n1:n2], send_kv)

    each_peer(lambda d, c: move_seg(d, c).wait())

    spot = lax.broadcasted_iota(jnp.int32, (tok, HD), 1)

    @pl.loop(0, blocks)
    def _(b):
        row = segs[b]
        across = jnp.broadcast_to(row[0:1, :], (tok, tok))
        down = jnp.transpose(across)
        q_mask[b] = jnp.where(spot == down, 1.0, 0.0).astype(jnp.bfloat16)
        k_mask[b] = jnp.where((spot < REQ_G) & (spot != down), FAR, 0.0).astype(jnp.bfloat16)

    @pl.when(lower)
    def _():
        for copy in hop_down():
            copy.wait_recv()
        hop_mirror_last().wait()
        for k in range(1, n_y):
            start(hop_y(1, k))

    @pl.when(upper)
    def _():
        for copy in hop_down():
            copy.wait_send()

    some(order[n2:], send_kv)
    own_text.wait()

    @pl.when(lower)
    def _():
        for half in range(n_hi):
            for k in range(1, n_y):
                wait(hop_y(half, k))
        to_scalars = pltpu.make_async_copy(meta_y, meta_sm, local_sem.at[3])
        to_scalars.start()
        to_scalars.wait()
        per_x = n_hi * REQ_G
        to_x = lax.rem(gx + lax.div(lane, per_x), n_x)
        to_hi = lax.rem(lax.div(lane, REQ_G), n_hi)
        wanted = member(to_hi, to_x, gy) * REQ_G + lax.rem(lane, REQ_G)
        wanted = jnp.where(lane < n_x * per_x, wanted, -1)
        at, lens = jnp.zeros((8, 128), jnp.int32), jnp.zeros((8, 128), jnp.int32)
        for b in range(n_hi * n_y):
            for r in range(REQ_G):
                hit = wanted == meta_sm[b, 0, r]
                at = jnp.where(hit, b * REQ_G + r, at)
                lens = jnp.where(hit, meta_sm[b, 0, REQ_G + r], lens)
        picks[...] = at
        meta_xs[...] = lens
        to_scalars = pltpu.make_async_copy(picks, picks_sm, local_sem.at[3])
        to_scalars.start()
        to_scalars.wait()
        for k in range(n_x):
            for j in range(per_x):
                text_xs[k, j] = text_y[picks_sm[0, k * per_x + j]]
        for k in range(1, n_x):
            start(hop_x(k))

    some(order[:4 * n_sect], send_q)

    @pl.when(lower)
    def _():
        for k in range(1, n_x):
            wait(hop_x(k))
        text_x[0] = text_xs[0]
        meta_x[0] = meta_xs[...]
        to_scalars = pltpu.make_async_copy(meta_x, meta_xm, local_sem.at[3])
        to_scalars.start()
        to_scalars.wait()
        for half, (text_to, meta_to) in enumerate(((text_own, meta_own), (text_far, meta_far))):
            lens = jnp.zeros((8, 128), jnp.int32)
            for j in range(REQ_G):
                at_x, count = jnp.int32(0), jnp.int32(0)
                for k in range(n_x):
                    here = meta_xm[k, 0, (k * n_hi + half) * REQ_G + j]
                    at_x = jnp.where(here > 0, k, at_x)
                    count = jnp.where(here > 0, here, count)
                text_to[j] = text_x[at_x, half * REQ_G + j]
                lens = jnp.where(lane == j, count, lens)
            meta_to[...] = lens
        pl.semaphore_wait(far_in, 1)
        start(hop_up())

    some(order[4 * n_sect:], send_q)

    @pl.when(upper)
    def _():
        for copy in hop_up():
            copy.wait_recv()

    to_scalars = pltpu.make_async_copy(meta_own, meta_own_sm, local_sem.at[4])
    to_scalars.start()
    to_scalars.wait()

    place = lax.broadcasted_iota(jnp.int32, (txt, HD), 0)
    spot_t = lax.broadcasted_iota(jnp.int32, (txt, HD), 1)
    for j in range(REQ_G):
        block, part = blocks + (j * txt) // tok, pl.ds((j * txt) % tok, txt)
        kv[block, 0, part] = text_own[j, 0]
        kv[block, 1, part] = text_own[j, 1]
        live = (spot_t == j) & (place < meta_own_sm[0, j])
        k_mask[block, part] = jnp.where((spot_t < REQ_G) & ~live, FAR, 0.0).astype(jnp.bfloat16)

    own_kv.wait()
    own_q.wait()
    each_peer(lambda d, c: move_kv(d, c).wait())

    factor = LOG2E / HD ** 0.5
    pair = n_sect * tok

    def attend(d):
        both = pl.ds(d * n_sect, n_sect)
        score[...] = lax.dot_general(
            jnp.concatenate([qb[both].reshape(pair, HD), q_mask[both].reshape(pair, HD)], axis=1),
            jnp.concatenate([kv[:, 0].reshape(keys, HD), k_mask[...].reshape(keys, HD)], axis=1),
            (((1,), (1,)), ((), ())), preferred_element_type=jnp.float32)
        top = jnp.max(score[...], axis=1, keepdims=True)
        prob[...] = jnp.exp2((score[...] - top) * factor).astype(jnp.bfloat16)
        mixed = jnp.dot(
            prob[...], jnp.concatenate([kv[:, 1].reshape(keys, HD), jnp.ones((keys, HD), jnp.bfloat16)], axis=1),
            preferred_element_type=jnp.float32)
        ob[both] = (mixed[:, :HD] / mixed[:, HD:]).astype(jnp.bfloat16).reshape(n_sect, tok, HD)

    for c in range(1, n_sect):
        move_q(0, c).wait()
    attend(0)
    for c in range(1, n_sect):
        move_o(0, c).start()

    @pl.loop(1, n_seq)
    def _(i):
        d = nth(i)
        for c in range(n_sect):
            move_q(d, c).wait()
        attend(d)
        for c in range(n_sect):
            move_o(d, c).start()

    @pl.when(lower)
    def _():
        for copy in hop_up():
            copy.wait_send()

    out_ref[:, columns(0, 0)] = ob[0]

    def finish(d, c):
        move_o(d, c).wait()
        out_ref[:, columns(d, c)] = landed[d * n_sect + c]

    each_peer(finish)


def local(mesh, qkv_img, img_seg, text_kv, txt_len, req_slot):
    n_seq, n_sect = mesh.shape["seq"], mesh.shape["sect"]
    n_hi, n_x, n_y = GRID
    blocks = n_seq * n_sect
    tok, width = qkv_img.shape[1], qkv_img.shape[3]
    txt = text_kv.shape[2]
    keys = blocks * tok + REQ_G * txt
    x = jnp.transpose(qkv_img[0], (1, 0, 2))
    dma = pltpu.SemaphoreType.DMA
    bf16, i32 = jnp.bfloat16, jnp.int32
    out = pl.pallas_call(
        functools.partial(kernel, (n_seq, n_sect, n_hi, n_x, n_y)),
        out_shape=jax.ShapeDtypeStruct((tok, width), bf16),
        in_specs=[
            pl.BlockSpec(memory_space=pl.ANY),
            pl.BlockSpec(memory_space=pl.ANY),
            pl.BlockSpec(memory_space=pl.ANY),
            pl.BlockSpec(memory_space=pl.ANY),
            pl.BlockSpec(memory_space=pl.ANY),
        ],
        out_specs=pl.BlockSpec(memory_space=pltpu.VMEM),
        scratch_shapes=[
            pltpu.VMEM((keys // tok, 2, tok, HD), bf16),
            pltpu.VMEM((keys // tok, tok, HD), bf16),
            pltpu.VMEM((blocks, tok, HD), bf16),
            pltpu.VMEM((blocks, tok, HD), bf16),
            pltpu.VMEM((blocks, tok, HD), bf16),
            pltpu.VMEM((blocks, tok, HD), bf16),
            pltpu.VMEM((n_sect * tok, keys), jnp.float32),
            pltpu.VMEM((n_sect * tok, keys), bf16),
            pltpu.VMEM((8, tok), i32),
            pltpu.VMEM((blocks, 8, tok), i32),
            pltpu.VMEM((REQ_G, 2, txt, HD), bf16),
            pltpu.VMEM((n_hi * n_y * REQ_G, 2, txt, HD), bf16),
            pltpu.VMEM((n_x, n_hi * REQ_G, 2, txt, HD), bf16),
            pltpu.VMEM((n_x, n_hi * REQ_G, 2, txt, HD), bf16),
            pltpu.VMEM((REQ_G, 2, txt, HD), bf16),
            pltpu.VMEM((REQ_G, 2, txt, HD), bf16),
            pltpu.VMEM((8, 128), i32),
            pltpu.VMEM((8, 128), i32),
            pltpu.VMEM((n_hi * n_y, 8, 128), i32),
            pltpu.VMEM((8, 128), i32),
            pltpu.VMEM((8, 128), i32),
            pltpu.VMEM((n_x, 8, 128), i32),
            pltpu.VMEM((8, 128), i32),
            pltpu.VMEM((8, 128), i32),
            pltpu.SMEM((n_hi * n_y, 8, 128), i32),
            pltpu.SMEM((8, 128), i32),
            pltpu.SMEM((n_x, 8, 128), i32),
            pltpu.SMEM((8, 128), i32),
            pltpu.SMEM((REQ_G,), i32),
            pltpu.SMEM((REQ_G,), i32),
            pltpu.VMEM((1, tok), i32),
            dma((8,)),
            pltpu.SemaphoreType.REGULAR,
            dma((blocks,)), dma((blocks,)),
            dma((blocks,)), dma((blocks,)),
            dma((blocks,)), dma((blocks,)),
            dma((blocks,)), dma((blocks,)),
            dma((2,)), dma((2,)),
            dma((2,)), dma((2,)),
            dma((2,)), dma((2,)),
            dma((2, n_hi, n_y)), dma((2, n_hi, n_y)),
            dma((2, n_x)), dma((2, n_x)),
            dma((2,)), dma((2,)),
        ],
        compiler_params=pltpu.CompilerParams(
            collective_id=0, has_side_effects=True, vmem_limit_bytes=63 * 1024 * 1024),
        name="routed_attention",
    )(req_slot, txt_len, x, img_seg, text_kv)
    return out[None]


def solution(mesh):
    return jax.shard_map(
        functools.partial(local, mesh),
        mesh=mesh,
        in_specs=(
            P("grp", ("sect", "seq"), None, None),
            P("grp", ("sect", "seq")),
            P("grp", None, None, ("sect", "seq")),
            P("grp"),
            P("grp"),
        ),
        out_specs=P("grp", ("sect", "seq"), None),
        check_vma=False,
    )
```

```python
import functools

import jax
import jax.numpy as jnp
from jax import lax
from jax.experimental import pallas as pl
from jax.experimental.pallas import tpu as pltpu
from jax.sharding import PartitionSpec as P

HD = 128
REQ_G = 4
GRID = (2, 4, 4)
SPLIT = 3
MESH = pl.DeviceIdType.MESH

FAR = -2097152.0
LOG2E = 1.4426950408889634


def kernel(
    dims,
    slot_ref, len_ref, x_ref, seg_ref, text_ref,
    out_ref,
    kv, k_mask, qb, q_mask, ob, landed, score, prob, seg_send, segs,
    text_in, text_y, text_xs, text_x, text_far, text_own,
    meta_send, meta_in, meta_y, picks, meta_xs, meta_x, meta_far, meta_own,
    meta_sm, picks_sm, meta_xm, meta_own_sm, slots, counts, seg_row,
    local_sem, far_in, rounds, seg_ss, seg_rs, kv_ss, kv_rs, q_ss, q_rs, o_ss, o_rs,
    ta_s, ta_r, tb_s, tb_r, td_s, td_r, ty_s, ty_r, tx_s, tx_r, tc_s, tc_r,
):
    n_seq, n_sect, n_hi, n_x, n_y = dims
    blocks = n_seq * n_sect
    tok = x_ref.shape[1]
    img = blocks * tok
    txt = text_ref.shape[2]
    keys = img + REQ_G * txt
    sect, grp, seq = lax.axis_index("sect"), lax.axis_index("grp"), lax.axis_index("seq")
    z_hi, gx, gy = lax.div(grp, n_x * n_y), lax.rem(lax.div(grp, n_y), n_x), lax.rem(grp, n_y)

    def chip_at(d):
        total, unit = 0, 1
        while unit < n_seq:
            bit = (d // unit) % 2 if isinstance(d, int) else lax.div(d, unit)
            total = total + unit * lax.rem(lax.div(seq, unit) + bit, 2)
            unit *= 2
        return total

    def core_at(c):
        return lax.rem(sect + c, n_sect)

    def columns(d, c):
        chip = chip_at(d)
        head = core_at(c) * n_seq + chip + z_hi * (n_seq - 1 - 2 * chip)
        return pl.ds(pl.multiple_of(head * HD, HD), HD)

    def peer(d, c):
        return {"sect": core_at(c), "grp": grp, "seq": chip_at(d)}

    def member(hi, x, y):
        return (hi * n_x + x) * n_y + y

    far = {"sect": sect, "grp": member(n_hi - 1 - z_hi, gx, gy), "seq": n_seq - 1 - seq}

    def along_y(k):
        return {"sect": sect, "grp": member(z_hi, gx, lax.rem(gy + k, n_y)), "seq": seq}

    def along_x(k):
        return {"sect": sect, "grp": member(z_hi, lax.rem(gx + k, n_x), gy), "seq": seq}

    lower, upper = z_hi == 0, z_hi == 1

    def nth(i):
        return n_seq // 2 + (2 * (i % 2) - 1) * (i // 2) if isinstance(i, int) else (
            n_seq // 2 + (2 * lax.rem(i, 2) - 1) * lax.div(i, 2))

    order = [(d, c) for a, b in ((4, 3), (5, 2), (6, 1)) for c in range(n_sect) for d in (a, b)] + [(7, 0), (7, 1)] + [(0, c) for c in range(1, n_sect)]

    def some(places, body):
        for d, c in places:
            body(d, c)

    def each_peer(body):
        @pl.loop(1, n_seq)
        def _(i):
            for c in range(n_sect):
                body(nth(i), c)

        for c in range(1, n_sect):
            body(0, c)

    small = (
        pltpu.make_async_copy(slot_ref, slots, local_sem.at[5]),
        pltpu.make_async_copy(len_ref, counts, local_sem.at[6]),
        pltpu.make_async_copy(seg_ref, seg_row, local_sem.at[7]),
    )
    for copy in small:
        copy.start()

    barrier = pltpu.get_barrier_semaphore()

    def greet(device):
        pl.semaphore_signal(barrier, inc=1, device_id=device, device_id_type=MESH)

    near = [(n_seq - 1, 0), (0, 1)] + [(1 << b, 0) for b in range(n_seq.bit_length() - 2)]
    some(near, lambda d, c: greet(peer(d, c)))

    @pl.when(lower)
    def _():
        for k in range(1, n_y):
            greet(along_y(k))
        for k in range(1, n_x):
            greet(along_x(k))
        greet(far)

    for copy in small:
        copy.wait()
    lane = lax.broadcasted_iota(jnp.int32, (8, 128), 1)
    meta = jnp.zeros((8, 128), jnp.int32)
    for r in range(REQ_G):
        meta = jnp.where(lane == r, slots[r], meta)
        meta = jnp.where(lane == REQ_G + r, counts[r], meta)
    meta_send[...] = meta
    seg_send[...] = jnp.broadcast_to(seg_row[...], (8, tok))
    segs[0] = jnp.broadcast_to(seg_row[...], (8, tok))

    @pl.when(lower)
    def _():
        pl.semaphore_wait(barrier, len(near) + n_y - 1 + n_x - 1)

    @pl.when(upper)
    def _():
        pl.semaphore_wait(barrier, len(near) + 1)
        pl.semaphore_signal(far_in, inc=1, device_id=far, device_id_type=MESH)

    def remote(src, dst, ss, rs, device):
        return pltpu.make_async_remote_copy(
            src_ref=src, dst_ref=dst, send_sem=ss, recv_sem=rs, device_id=device, device_id_type=MESH)

    def start(copies):
        for copy in copies:
            copy.start()

    def wait(copies):
        for copy in copies:
            copy.wait()

    def hop_mirror():
        mate = peer(n_seq - 1, 0)
        return (
            remote(meta_send, meta_in, ta_s.at[0], ta_r.at[0], mate),
            remote(
                text_ref.at[pl.ds(0, SPLIT)], text_in.at[pl.ds(0, SPLIT)],
                ta_s.at[1], ta_r.at[1], mate),
        )

    def requests(half, k):
        return pl.ds((half * n_y + k) * REQ_G, REQ_G)

    def hop_down():
        return (
            remote(meta_in, meta_y.at[n_y], tb_s.at[0], tb_r.at[0], far),
            remote(
                text_in.at[pl.ds(0, SPLIT)], text_y.at[pl.ds(n_y * REQ_G, SPLIT)],
                tb_s.at[1], tb_r.at[1], far),
        )

    late = pl.ds(SPLIT, REQ_G - SPLIT)

    def hop_down_first():
        return remote(text_ref.at[late], text_in.at[late], td_s.at[0], td_r.at[0], far)

    def hop_mirror_last():
        return remote(
            text_in.at[late], text_y.at[pl.ds(n_y * REQ_G + SPLIT, REQ_G - SPLIT)],
            td_s.at[1], td_r.at[1], peer(n_seq - 1, 0))

    def hop_y(half, k):
        meta_src = meta_y.at[n_y] if half else meta_send
        text_src = text_y.at[requests(1, 0)] if half else text_ref
        return (
            remote(meta_src, meta_y.at[half * n_y + k], ty_s.at[0, half, k], ty_r.at[0, half, k], along_y(k)),
            remote(text_src, text_y.at[requests(half, k)], ty_s.at[1, half, k], ty_r.at[1, half, k], along_y(k)),
        )

    def hop_x(k):
        return (
            remote(meta_xs, meta_x.at[k], tx_s.at[0, k], tx_r.at[0, k], along_x(k)),
            remote(text_xs.at[k], text_x.at[k], tx_s.at[1, k], tx_r.at[1, k], along_x(k)),
        )

    def hop_up():
        return (
            remote(meta_far, meta_own, tc_s.at[0], tc_r.at[0], far),
            remote(text_far, text_own, tc_s.at[1], tc_r.at[1], far),
        )

    def move_seg(d, c):
        at = d * n_sect + c
        return remote(seg_send, segs.at[at], seg_ss.at[at], seg_rs.at[at], peer(d, c))

    def move_kv(d, c):
        at = d * n_sect + c
        return remote(x_ref.at[pl.ds(1, 2), :, columns(d, c)], kv.at[at], kv_ss.at[at], kv_rs.at[at], peer(d, c))

    def move_q(d, c):
        at = d * n_sect + c
        return remote(x_ref.at[0, :, columns(d, c)], qb.at[at], q_ss.at[at], q_rs.at[at], peer(d, c))

    def move_o(d, c):
        at = d * n_sect + c
        return remote(ob.at[at], landed.at[at], o_ss.at[at], o_rs.at[at], peer(d, c))

    def send_kv(d, c):
        move_kv(d, c).start()

    def send_q(d, c):
        move_q(d, c).start()

    n1, n2 = 2 * n_sect - 1, 5 * n_sect - 1

    @pl.when(upper)
    def _():
        start(hop_mirror())
        hop_down_first().start()

    some(near[:1], send_kv)
    for r, (d, c) in enumerate(near[1:]):
        pl.semaphore_signal(rounds.at[r], inc=1, device_id=peer(d, c), device_id_type=MESH)
        pl.semaphore_wait(rounds.at[r], 1)
    q_order = order
    order = [place for place in order if place not in near[:1]]

    some(order[:n_sect], send_kv)
    each_peer(lambda d, c: move_seg(d, c).start())
    some(order[n_sect:n1], send_kv)

    @pl.when(lower)
    def _():
        for k in range(1, n_y):
            start(hop_y(0, k))

    own_text = pltpu.make_async_copy(text_ref, text_y.at[requests(0, 0)], local_sem.at[0])
    own_text.start()
    own_kv = pltpu.make_async_copy(x_ref.at[pl.ds(1, 2), :, columns(0, 0)], kv.at[0], local_sem.at[1])
    own_kv.start()
    own_q = pltpu.make_async_copy(x_ref.at[0, :, columns(0, 0)], qb.at[0], local_sem.at[2])
    own_q.start()
    meta_y[0] = meta

    @pl.when(upper)
    def _():
        wait(hop_mirror())
        start(hop_down())
        hop_down_first().wait_send()

    @pl.when(lower)
    def _():
        hop_down_first().wait_recv()
        hop_mirror_last().start()

    some(order[n1:n2], send_kv)

    each_peer(lambda d, c: move_seg(d, c).wait())

    spot = lax.broadcasted_iota(jnp.int32, (tok, HD), 1)

    @pl.loop(0, blocks)
    def _(b):
        row = segs[b]
        across = jnp.broadcast_to(row[0:1, :], (tok, tok))
        down = jnp.transpose(across)
        q_mask[b] = jnp.where(spot == down, 1.0, 0.0).astype(jnp.bfloat16)
        k_mask[b] = jnp.where((spot < REQ_G) & (spot != down), FAR, 0.0).astype(jnp.bfloat16)

    @pl.when(lower)
    def _():
        for copy in hop_down():
            copy.wait_recv()
        hop_mirror_last().wait()
        for k in range(1, n_y):
            start(hop_y(1, k))

    @pl.when(upper)
    def _():
        for copy in hop_down():
            copy.wait_send()

    some(order[n2:], send_kv)
    own_text.wait()

    @pl.when(lower)
    def _():
        for half in range(n_hi):
            for k in range(1, n_y):
                wait(hop_y(half, k))
        to_scalars = pltpu.make_async_copy(meta_y, meta_sm, local_sem.at[3])
        to_scalars.start()
        to_scalars.wait()
        per_x = n_hi * REQ_G
        to_x = lax.rem(gx + lax.div(lane, per_x), n_x)
        to_hi = lax.rem(lax.div(lane, REQ_G), n_hi)
        wanted = member(to_hi, to_x, gy) * REQ_G + lax.rem(lane, REQ_G)
        wanted = jnp.where(lane < n_x * per_x, wanted, -1)
        at, lens = jnp.zeros((8, 128), jnp.int32), jnp.zeros((8, 128), jnp.int32)
        for b in range(n_hi * n_y):
            for r in range(REQ_G):
                hit = wanted == meta_sm[b, 0, r]
                at = jnp.where(hit, b * REQ_G + r, at)
                lens = jnp.where(hit, meta_sm[b, 0, REQ_G + r], lens)
        picks[...] = at
        meta_xs[...] = lens
        to_scalars = pltpu.make_async_copy(picks, picks_sm, local_sem.at[3])
        to_scalars.start()
        to_scalars.wait()
        for k in range(n_x):
            for j in range(per_x):
                text_xs[k, j] = text_y[picks_sm[0, k * per_x + j]]
        for k in range(1, n_x):
            start(hop_x(k))

    some(q_order[:4 * n_sect], send_q)

    @pl.when(lower)
    def _():
        for k in range(1, n_x):
            wait(hop_x(k))
        text_x[0] = text_xs[0]
        meta_x[0] = meta_xs[...]
        to_scalars = pltpu.make_async_copy(meta_x, meta_xm, local_sem.at[3])
        to_scalars.start()
        to_scalars.wait()
        for half, (text_to, meta_to) in enumerate(((text_own, meta_own), (text_far, meta_far))):
            lens = jnp.zeros((8, 128), jnp.int32)
            for j in range(REQ_G):
                at_x, count = jnp.int32(0), jnp.int32(0)
                for k in range(n_x):
                    here = meta_xm[k, 0, (k * n_hi + half) * REQ_G + j]
                    at_x = jnp.where(here > 0, k, at_x)
                    count = jnp.where(here > 0, here, count)
                text_to[j] = text_x[at_x, half * REQ_G + j]
                lens = jnp.where(lane == j, count, lens)
            meta_to[...] = lens
        pl.semaphore_wait(far_in, 1)
        start(hop_up())

    some(q_order[4 * n_sect:], send_q)

    @pl.when(upper)
    def _():
        for copy in hop_up():
            copy.wait_recv()

    to_scalars = pltpu.make_async_copy(meta_own, meta_own_sm, local_sem.at[4])
    to_scalars.start()
    to_scalars.wait()

    place = lax.broadcasted_iota(jnp.int32, (txt, HD), 0)
    spot_t = lax.broadcasted_iota(jnp.int32, (txt, HD), 1)
    for j in range(REQ_G):
        block, part = blocks + (j * txt) // tok, pl.ds((j * txt) % tok, txt)
        kv[block, 0, part] = text_own[j, 0]
        kv[block, 1, part] = text_own[j, 1]
        live = (spot_t == j) & (place < meta_own_sm[0, j])
        k_mask[block, part] = jnp.where((spot_t < REQ_G) & ~live, FAR, 0.0).astype(jnp.bfloat16)

    own_kv.wait()
    own_q.wait()
    each_peer(lambda d, c: move_kv(d, c).wait())

    factor = LOG2E / HD ** 0.5
    pair = n_sect * tok

    def attend(d):
        both = pl.ds(d * n_sect, n_sect)
        score[...] = lax.dot_general(
            jnp.concatenate([qb[both].reshape(pair, HD), q_mask[both].reshape(pair, HD)], axis=1),
            jnp.concatenate([kv[:, 0].reshape(keys, HD), k_mask[...].reshape(keys, HD)], axis=1),
            (((1,), (1,)), ((), ())), preferred_element_type=jnp.float32)
        top = jnp.max(score[...], axis=1, keepdims=True)
        prob[...] = jnp.exp2((score[...] - top) * factor).astype(jnp.bfloat16)
        mixed = jnp.dot(
            prob[...], jnp.concatenate([kv[:, 1].reshape(keys, HD), jnp.ones((keys, HD), jnp.bfloat16)], axis=1),
            preferred_element_type=jnp.float32)
        ob[both] = (mixed[:, :HD] / mixed[:, HD:]).astype(jnp.bfloat16).reshape(n_sect, tok, HD)

    @pl.loop(1, n_seq)
    def _(i):
        d = nth(i)
        for c in range(n_sect):
            move_q(d, c).wait_recv()
        attend(d)
        for c in range(n_sect):
            move_o(d, c).start()

    for c in range(1, n_sect):
        move_q(0, c).wait_recv()
    attend(0)
    for c in range(1, n_sect):
        move_o(0, c).start()

    @pl.when(lower)
    def _():
        for copy in hop_up():
            copy.wait_send()

    out_ref[:, columns(0, 0)] = ob[0]

    def finish(d, c):
        move_q(d, c).wait_send()
        move_o(d, c).wait()
        out_ref[:, columns(d, c)] = landed[d * n_sect + c]

    each_peer(finish)


def local(mesh, qkv_img, img_seg, text_kv, txt_len, req_slot):
    n_seq, n_sect = mesh.shape["seq"], mesh.shape["sect"]
    n_hi, n_x, n_y = GRID
    blocks = n_seq * n_sect
    tok, width = qkv_img.shape[1], qkv_img.shape[3]
    txt = text_kv.shape[2]
    keys = blocks * tok + REQ_G * txt
    x = jnp.transpose(qkv_img[0], (1, 0, 2))
    dma = pltpu.SemaphoreType.DMA
    bf16, i32 = jnp.bfloat16, jnp.int32
    out = pl.pallas_call(
        functools.partial(kernel, (n_seq, n_sect, n_hi, n_x, n_y)),
        out_shape=jax.ShapeDtypeStruct((tok, width), bf16),
        in_specs=[
            pl.BlockSpec(memory_space=pl.ANY),
            pl.BlockSpec(memory_space=pl.ANY),
            pl.BlockSpec(memory_space=pl.ANY),
            pl.BlockSpec(memory_space=pl.ANY),
            pl.BlockSpec(memory_space=pl.ANY),
        ],
        out_specs=pl.BlockSpec(memory_space=pltpu.VMEM),
        scratch_shapes=[
            pltpu.VMEM((keys // tok, 2, tok, HD), bf16),
            pltpu.VMEM((keys // tok, tok, HD), bf16),
            pltpu.VMEM((blocks, tok, HD), bf16),
            pltpu.VMEM((blocks, tok, HD), bf16),
            pltpu.VMEM((blocks, tok, HD), bf16),
            pltpu.VMEM((blocks, tok, HD), bf16),
            pltpu.VMEM((n_sect * tok, keys), jnp.float32),
            pltpu.VMEM((n_sect * tok, keys), bf16),
            pltpu.VMEM((8, tok), i32),
            pltpu.VMEM((blocks, 8, tok), i32),
            pltpu.VMEM((REQ_G, 2, txt, HD), bf16),
            pltpu.VMEM((n_hi * n_y * REQ_G, 2, txt, HD), bf16),
            pltpu.VMEM((n_x, n_hi * REQ_G, 2, txt, HD), bf16),
            pltpu.VMEM((n_x, n_hi * REQ_G, 2, txt, HD), bf16),
            pltpu.VMEM((REQ_G, 2, txt, HD), bf16),
            pltpu.VMEM((REQ_G, 2, txt, HD), bf16),
            pltpu.VMEM((8, 128), i32),
            pltpu.VMEM((8, 128), i32),
            pltpu.VMEM((n_hi * n_y, 8, 128), i32),
            pltpu.VMEM((8, 128), i32),
            pltpu.VMEM((8, 128), i32),
            pltpu.VMEM((n_x, 8, 128), i32),
            pltpu.VMEM((8, 128), i32),
            pltpu.VMEM((8, 128), i32),
            pltpu.SMEM((n_hi * n_y, 8, 128), i32),
            pltpu.SMEM((8, 128), i32),
            pltpu.SMEM((n_x, 8, 128), i32),
            pltpu.SMEM((8, 128), i32),
            pltpu.SMEM((REQ_G,), i32),
            pltpu.SMEM((REQ_G,), i32),
            pltpu.VMEM((1, tok), i32),
            dma((8,)),
            pltpu.SemaphoreType.REGULAR,
            pltpu.SemaphoreType.REGULAR((3,)),
            dma((blocks,)), dma((blocks,)),
            dma((blocks,)), dma((blocks,)),
            dma((blocks,)), dma((blocks,)),
            dma((blocks,)), dma((blocks,)),
            dma((2,)), dma((2,)),
            dma((2,)), dma((2,)),
            dma((2,)), dma((2,)),
            dma((2, n_hi, n_y)), dma((2, n_hi, n_y)),
            dma((2, n_x)), dma((2, n_x)),
            dma((2,)), dma((2,)),
        ],
        compiler_params=pltpu.CompilerParams(
            collective_id=0, has_side_effects=True, vmem_limit_bytes=63 * 1024 * 1024),
        name="routed_attention",
    )(req_slot, txt_len, x, img_seg, text_kv)
    return out[None]


def solution(mesh):
    return jax.shard_map(
        functools.partial(local, mesh),
        mesh=mesh,
        in_specs=(
            P("grp", ("sect", "seq"), None, None),
            P("grp", ("sect", "seq")),
            P("grp", None, None, ("sect", "seq")),
            P("grp"),
            P("grp"),
        ),
        out_specs=P("grp", ("sect", "seq"), None),
        check_vma=False,
    )
```

```python
import functools

import jax
import jax.numpy as jnp
from jax import lax
from jax.experimental import pallas as pl
from jax.experimental.pallas import tpu as pltpu
from jax.sharding import PartitionSpec as P

HD = 128
REQ_G = 4
GRID = (2, 4, 4)
SPLIT = 4
MESH = pl.DeviceIdType.MESH

FAR = -2097152.0
LOG2E = 1.4426950408889634


def kernel(
    dims,
    slot_ref, len_ref, x_ref, seg_ref, text_ref,
    out_ref,
    kv, k_mask, qb, q_mask, ob, landed, score, prob, seg_send, segs,
    text_in, text_y, text_xs, text_x, text_far, text_own,
    meta_send, meta_in, meta_y, picks, meta_xs, meta_x, meta_far, meta_own,
    meta_sm, picks_sm, meta_xm, meta_own_sm, slots, counts, seg_row,
    local_sem, far_in, rounds, seg_ss, seg_rs, kv_ss, kv_rs, q_ss, q_rs, o_ss, o_rs,
    ta_s, ta_r, tb_s, tb_r, ty_s, ty_r, tx_s, tx_r, tc_s, tc_r,
):
    n_seq, n_sect, n_hi, n_x, n_y = dims
    blocks = n_seq * n_sect
    tok = x_ref.shape[1]
    img = blocks * tok
    txt = text_ref.shape[2]
    keys = img + REQ_G * txt
    sect, grp, seq = lax.axis_index("sect"), lax.axis_index("grp"), lax.axis_index("seq")
    z_hi, gx, gy = lax.div(grp, n_x * n_y), lax.rem(lax.div(grp, n_y), n_x), lax.rem(grp, n_y)

    def chip_at(d):
        total, unit = 0, 1
        while unit < n_seq:
            bit = (d // unit) % 2 if isinstance(d, int) else lax.div(d, unit)
            total = total + unit * lax.rem(lax.div(seq, unit) + bit, 2)
            unit *= 2
        return total

    def core_at(c):
        return lax.rem(sect + c, n_sect)

    def columns(d, c):
        chip = chip_at(d)
        head = core_at(c) * n_seq + chip + z_hi * (n_seq - 1 - 2 * chip)
        return pl.ds(pl.multiple_of(head * HD, HD), HD)

    def peer(d, c):
        return {"sect": core_at(c), "grp": grp, "seq": chip_at(d)}

    def member(hi, x, y):
        return (hi * n_x + x) * n_y + y

    far = {"sect": sect, "grp": member(n_hi - 1 - z_hi, gx, gy), "seq": n_seq - 1 - seq}

    def along_y(k):
        return {"sect": sect, "grp": member(z_hi, gx, lax.rem(gy + k, n_y)), "seq": seq}

    def along_x(k):
        return {"sect": sect, "grp": member(z_hi, lax.rem(gx + k, n_x), gy), "seq": seq}

    lower, upper = z_hi == 0, z_hi == 1

    def nth(i):
        return n_seq // 2 + (2 * (i % 2) - 1) * (i // 2) if isinstance(i, int) else (
            n_seq // 2 + (2 * lax.rem(i, 2) - 1) * lax.div(i, 2))

    order = [(d, c) for a, b in ((4, 3), (5, 2), (6, 1)) for c in range(n_sect) for d in (a, b)] + [(7, 0), (7, 1)] + [(0, c) for c in range(1, n_sect)]

    def some(places, body):
        for d, c in places:
            body(d, c)

    def each_peer(body):
        @pl.loop(1, n_seq)
        def _(i):
            for c in range(n_sect):
                body(nth(i), c)

        for c in range(1, n_sect):
            body(0, c)

    small = (
        pltpu.make_async_copy(slot_ref, slots, local_sem.at[5]),
        pltpu.make_async_copy(len_ref, counts, local_sem.at[6]),
        pltpu.make_async_copy(seg_ref, seg_row, local_sem.at[7]),
    )
    for copy in small:
        copy.start()

    barrier = pltpu.get_barrier_semaphore()

    def greet(device):
        pl.semaphore_signal(barrier, inc=1, device_id=device, device_id_type=MESH)

    near = [(n_seq - 1, 0), (0, 1)] + [(1 << b, 0) for b in range(n_seq.bit_length() - 2)]
    some(near, lambda d, c: greet(peer(d, c)))

    @pl.when(lower)
    def _():
        for k in range(1, n_y):
            greet(along_y(k))
        for k in range(1, n_x):
            greet(along_x(k))
        greet(far)

    for copy in small:
        copy.wait()
    lane = lax.broadcasted_iota(jnp.int32, (8, 128), 1)
    meta = jnp.zeros((8, 128), jnp.int32)
    for r in range(REQ_G):
        meta = jnp.where(lane == r, slots[r], meta)
        meta = jnp.where(lane == REQ_G + r, counts[r], meta)
    meta_send[...] = meta
    seg_send[...] = jnp.broadcast_to(seg_row[...], (8, tok))
    segs[0] = jnp.broadcast_to(seg_row[...], (8, tok))

    @pl.when(lower)
    def _():
        pl.semaphore_wait(barrier, len(near) + n_y - 1 + n_x - 1)

    @pl.when(upper)
    def _():
        pl.semaphore_wait(barrier, len(near) + 1)
        pl.semaphore_signal(far_in, inc=1, device_id=far, device_id_type=MESH)

    def remote(src, dst, ss, rs, device):
        return pltpu.make_async_remote_copy(
            src_ref=src, dst_ref=dst, send_sem=ss, recv_sem=rs, device_id=device, device_id_type=MESH)

    def start(copies):
        for copy in copies:
            copy.start()

    def wait(copies):
        for copy in copies:
            copy.wait()

    def hop_mirror():
        mate = peer(n_seq - 1, 0)
        return (
            remote(meta_send, meta_in, ta_s.at[0], ta_r.at[0], mate),
            remote(
                text_ref.at[pl.ds(0, SPLIT)], text_in.at[pl.ds(0, SPLIT)],
                ta_s.at[1], ta_r.at[1], mate),
        )

    def requests(half, k):
        return pl.ds((half * n_y + k) * REQ_G, REQ_G)

    def hop_down():
        return (
            remote(meta_in, meta_y.at[n_y], tb_s.at[0], tb_r.at[0], far),
            remote(
                text_in.at[pl.ds(0, SPLIT)], text_y.at[pl.ds(n_y * REQ_G, SPLIT)],
                tb_s.at[1], tb_r.at[1], far),
        )

    def hop_y(half, k):
        meta_src = meta_y.at[n_y] if half else meta_send
        text_src = text_y.at[requests(1, 0)] if half else text_ref
        return (
            remote(meta_src, meta_y.at[half * n_y + k], ty_s.at[0, half, k], ty_r.at[0, half, k], along_y(k)),
            remote(text_src, text_y.at[requests(half, k)], ty_s.at[1, half, k], ty_r.at[1, half, k], along_y(k)),
        )

    def hop_x(k):
        return (
            remote(meta_xs, meta_x.at[k], tx_s.at[0, k], tx_r.at[0, k], along_x(k)),
            remote(text_xs.at[k], text_x.at[k], tx_s.at[1, k], tx_r.at[1, k], along_x(k)),
        )

    def hop_up():
        return (
            remote(meta_far, meta_own, tc_s.at[0], tc_r.at[0], far),
            remote(text_far, text_own, tc_s.at[1], tc_r.at[1], far),
        )

    def move_seg(d, c):
        at = d * n_sect + c
        return remote(seg_send, segs.at[at], seg_ss.at[at], seg_rs.at[at], peer(d, c))

    def move_kv(d, c):
        at = d * n_sect + c
        return remote(x_ref.at[pl.ds(1, 2), :, columns(d, c)], kv.at[at], kv_ss.at[at], kv_rs.at[at], peer(d, c))

    def move_q(d, c):
        at = d * n_sect + c
        return remote(x_ref.at[0, :, columns(d, c)], qb.at[at], q_ss.at[at], q_rs.at[at], peer(d, c))

    def move_o(d, c):
        at = d * n_sect + c
        return remote(ob.at[at], landed.at[at], o_ss.at[at], o_rs.at[at], peer(d, c))

    def send_kv(d, c):
        move_kv(d, c).start()

    def send_q(d, c):
        move_q(d, c).start()

    n1, n2 = 2 * n_sect - 1, 5 * n_sect - 1

    @pl.when(upper)
    def _():
        start(hop_mirror())

    some(near[:1], send_kv)
    for r, (d, c) in enumerate(near[1:]):
        pl.semaphore_signal(rounds.at[r], inc=1, device_id=peer(d, c), device_id_type=MESH)
        pl.semaphore_wait(rounds.at[r], 1)
    q_order = order
    order = [place for place in order if place not in near[:1]]

    some(order[:n_sect], send_kv)
    each_peer(lambda d, c: move_seg(d, c).start())
    some(order[n_sect:n1], send_kv)

    @pl.when(lower)
    def _():
        for k in range(1, n_y):
            start(hop_y(0, k))

    own_text = pltpu.make_async_copy(text_ref, text_y.at[requests(0, 0)], local_sem.at[0])
    own_text.start()
    own_kv = pltpu.make_async_copy(x_ref.at[pl.ds(1, 2), :, columns(0, 0)], kv.at[0], local_sem.at[1])
    own_kv.start()
    own_q = pltpu.make_async_copy(x_ref.at[0, :, columns(0, 0)], qb.at[0], local_sem.at[2])
    own_q.start()
    meta_y[0] = meta

    @pl.when(upper)
    def _():
        wait(hop_mirror())
        start(hop_down())

    some(order[n1:n2], send_kv)

    each_peer(lambda d, c: move_seg(d, c).wait())

    spot = lax.broadcasted_iota(jnp.int32, (tok, HD), 1)

    @pl.loop(0, blocks)
    def _(b):
        row = segs[b]
        across = jnp.broadcast_to(row[0:1, :], (tok, tok))
        down = jnp.transpose(across)
        q_mask[b] = jnp.where(spot == down, 1.0, 0.0).astype(jnp.bfloat16)
        k_mask[b] = jnp.where((spot < REQ_G) & (spot != down), FAR, 0.0).astype(jnp.bfloat16)

    @pl.when(lower)
    def _():
        for copy in hop_down():
            copy.wait_recv()
        for k in range(1, n_y):
            start(hop_y(1, k))

    @pl.when(upper)
    def _():
        for copy in hop_down():
            copy.wait_send()

    some(order[n2:], send_kv)
    own_text.wait()

    @pl.when(lower)
    def _():
        for half in range(n_hi):
            for k in range(1, n_y):
                wait(hop_y(half, k))
        to_scalars = pltpu.make_async_copy(meta_y, meta_sm, local_sem.at[3])
        to_scalars.start()
        to_scalars.wait()
        per_x = n_hi * REQ_G
        to_x = lax.rem(gx + lax.div(lane, per_x), n_x)
        to_hi = lax.rem(lax.div(lane, REQ_G), n_hi)
        wanted = member(to_hi, to_x, gy) * REQ_G + lax.rem(lane, REQ_G)
        wanted = jnp.where(lane < n_x * per_x, wanted, -1)
        at, lens = jnp.zeros((8, 128), jnp.int32), jnp.zeros((8, 128), jnp.int32)
        for b in range(n_hi * n_y):
            for r in range(REQ_G):
                hit = wanted == meta_sm[b, 0, r]
                at = jnp.where(hit, b * REQ_G + r, at)
                lens = jnp.where(hit, meta_sm[b, 0, REQ_G + r], lens)
        picks[...] = at
        meta_xs[...] = lens
        to_scalars = pltpu.make_async_copy(picks, picks_sm, local_sem.at[3])
        to_scalars.start()
        to_scalars.wait()
        for k in range(n_x):
            for j in range(per_x):
                text_xs[k, j] = text_y[picks_sm[0, k * per_x + j]]
        for k in range(1, n_x):
            start(hop_x(k))

    some(q_order[:4 * n_sect], send_q)

    @pl.when(lower)
    def _():
        for k in range(1, n_x):
            wait(hop_x(k))
        text_x[0] = text_xs[0]
        meta_x[0] = meta_xs[...]
        to_scalars = pltpu.make_async_copy(meta_x, meta_xm, local_sem.at[3])
        to_scalars.start()
        to_scalars.wait()
        for half, (text_to, meta_to) in enumerate(((text_own, meta_own), (text_far, meta_far))):
            lens = jnp.zeros((8, 128), jnp.int32)
            for j in range(REQ_G):
                at_x, count = jnp.int32(0), jnp.int32(0)
                for k in range(n_x):
                    here = meta_xm[k, 0, (k * n_hi + half) * REQ_G + j]
                    at_x = jnp.where(here > 0, k, at_x)
                    count = jnp.where(here > 0, here, count)
                text_to[j] = text_x[at_x, half * REQ_G + j]
                lens = jnp.where(lane == j, count, lens)
            meta_to[...] = lens
        pl.semaphore_wait(far_in, 1)
        start(hop_up())

    some(q_order[4 * n_sect:], send_q)

    @pl.when(upper)
    def _():
        for copy in hop_up():
            copy.wait_recv()

    to_scalars = pltpu.make_async_copy(meta_own, meta_own_sm, local_sem.at[4])
    to_scalars.start()
    to_scalars.wait()

    place = lax.broadcasted_iota(jnp.int32, (txt, HD), 0)
    spot_t = lax.broadcasted_iota(jnp.int32, (txt, HD), 1)
    for j in range(REQ_G):
        block, part = blocks + (j * txt) // tok, pl.ds((j * txt) % tok, txt)
        kv[block, 0, part] = text_own[j, 0]
        kv[block, 1, part] = text_own[j, 1]
        live = (spot_t == j) & (place < meta_own_sm[0, j])
        k_mask[block, part] = jnp.where((spot_t < REQ_G) & ~live, FAR, 0.0).astype(jnp.bfloat16)

    own_kv.wait()
    own_q.wait()
    each_peer(lambda d, c: move_kv(d, c).wait())

    factor = LOG2E / HD ** 0.5
    pair = n_sect * tok

    def attend(d):
        both = pl.ds(d * n_sect, n_sect)
        score[...] = lax.dot_general(
            jnp.concatenate([qb[both].reshape(pair, HD), q_mask[both].reshape(pair, HD)], axis=1),
            jnp.concatenate([kv[:, 0].reshape(keys, HD), k_mask[...].reshape(keys, HD)], axis=1),
            (((1,), (1,)), ((), ())), preferred_element_type=jnp.float32)
        top = jnp.max(score[...], axis=1, keepdims=True)
        prob[...] = jnp.exp2((score[...] - top) * factor).astype(jnp.bfloat16)
        mixed = jnp.dot(
            prob[...], jnp.concatenate([kv[:, 1].reshape(keys, HD), jnp.ones((keys, HD), jnp.bfloat16)], axis=1),
            preferred_element_type=jnp.float32)
        ob[both] = (mixed[:, :HD] / mixed[:, HD:]).astype(jnp.bfloat16).reshape(n_sect, tok, HD)

    @pl.loop(1, n_seq)
    def _(i):
        d = nth(i)
        for c in range(n_sect):
            move_q(d, c).wait_recv()
        attend(d)
        for c in range(n_sect):
            move_o(d, c).start()

    for c in range(1, n_sect):
        move_q(0, c).wait_recv()
    attend(0)
    for c in range(1, n_sect):
        move_o(0, c).start()

    @pl.when(lower)
    def _():
        for copy in hop_up():
            copy.wait_send()

    out_ref[:, columns(0, 0)] = ob[0]

    def finish(d, c):
        move_q(d, c).wait_send()
        move_o(d, c).wait()
        out_ref[:, columns(d, c)] = landed[d * n_sect + c]

    each_peer(finish)


def local(mesh, qkv_img, img_seg, text_kv, txt_len, req_slot):
    n_seq, n_sect = mesh.shape["seq"], mesh.shape["sect"]
    n_hi, n_x, n_y = GRID
    blocks = n_seq * n_sect
    tok, width = qkv_img.shape[1], qkv_img.shape[3]
    txt = text_kv.shape[2]
    keys = blocks * tok + REQ_G * txt
    x = jnp.transpose(qkv_img[0], (1, 0, 2))
    dma = pltpu.SemaphoreType.DMA
    bf16, i32 = jnp.bfloat16, jnp.int32
    out = pl.pallas_call(
        functools.partial(kernel, (n_seq, n_sect, n_hi, n_x, n_y)),
        out_shape=jax.ShapeDtypeStruct((tok, width), bf16),
        in_specs=[
            pl.BlockSpec(memory_space=pl.ANY),
            pl.BlockSpec(memory_space=pl.ANY),
            pl.BlockSpec(memory_space=pl.ANY),
            pl.BlockSpec(memory_space=pl.ANY),
            pl.BlockSpec(memory_space=pl.ANY),
        ],
        out_specs=pl.BlockSpec(memory_space=pltpu.VMEM),
        scratch_shapes=[
            pltpu.VMEM((keys // tok, 2, tok, HD), bf16),
            pltpu.VMEM((keys // tok, tok, HD), bf16),
            pltpu.VMEM((blocks, tok, HD), bf16),
            pltpu.VMEM((blocks, tok, HD), bf16),
            pltpu.VMEM((blocks, tok, HD), bf16),
            pltpu.VMEM((blocks, tok, HD), bf16),
            pltpu.VMEM((n_sect * tok, keys), jnp.float32),
            pltpu.VMEM((n_sect * tok, keys), bf16),
            pltpu.VMEM((8, tok), i32),
            pltpu.VMEM((blocks, 8, tok), i32),
            pltpu.VMEM((REQ_G, 2, txt, HD), bf16),
            pltpu.VMEM((n_hi * n_y * REQ_G, 2, txt, HD), bf16),
            pltpu.VMEM((n_x, n_hi * REQ_G, 2, txt, HD), bf16),
            pltpu.VMEM((n_x, n_hi * REQ_G, 2, txt, HD), bf16),
            pltpu.VMEM((REQ_G, 2, txt, HD), bf16),
            pltpu.VMEM((REQ_G, 2, txt, HD), bf16),
            pltpu.VMEM((8, 128), i32),
            pltpu.VMEM((8, 128), i32),
            pltpu.VMEM((n_hi * n_y, 8, 128), i32),
            pltpu.VMEM((8, 128), i32),
            pltpu.VMEM((8, 128), i32),
            pltpu.VMEM((n_x, 8, 128), i32),
            pltpu.VMEM((8, 128), i32),
            pltpu.VMEM((8, 128), i32),
            pltpu.SMEM((n_hi * n_y, 8, 128), i32),
            pltpu.SMEM((8, 128), i32),
            pltpu.SMEM((n_x, 8, 128), i32),
            pltpu.SMEM((8, 128), i32),
            pltpu.SMEM((REQ_G,), i32),
            pltpu.SMEM((REQ_G,), i32),
            pltpu.VMEM((1, tok), i32),
            dma((8,)),
            pltpu.SemaphoreType.REGULAR,
            pltpu.SemaphoreType.REGULAR((3,)),
            dma((blocks,)), dma((blocks,)),
            dma((blocks,)), dma((blocks,)),
            dma((blocks,)), dma((blocks,)),
            dma((blocks,)), dma((blocks,)),
            dma((2,)), dma((2,)),
            dma((2,)), dma((2,)),
            dma((2, n_hi, n_y)), dma((2, n_hi, n_y)),
            dma((2, n_x)), dma((2, n_x)),
            dma((2,)), dma((2,)),
        ],
        compiler_params=pltpu.CompilerParams(
            collective_id=0, has_side_effects=True, vmem_limit_bytes=63 * 1024 * 1024),
        name="routed_attention",
    )(req_slot, txt_len, x, img_seg, text_kv)
    return out[None]


def solution(mesh):
    return jax.shard_map(
        functools.partial(local, mesh),
        mesh=mesh,
        in_specs=(
            P("grp", ("sect", "seq"), None, None),
            P("grp", ("sect", "seq")),
            P("grp", None, None, ("sect", "seq")),
            P("grp"),
            P("grp"),
        ),
        out_specs=P("grp", ("sect", "seq"), None),
        check_vma=False,
    )
```
